256 devices in a mesh: blk: 32 (over z, x_hi, core), tensor: 8 (over y, x_lo).
Axes of the slice: x: 4 (x_hi: 2, x_lo: 2; x = x_hi * 2 + x_lo), y: 4, z: 8, core: 2. Of those that a mesh axis runs over, the one named last changes fastest.
Arguments:
- inputs: bfloat16 [10240, 8192], P('blk'), may hold values from -96 to 96, as said below
- query_weight: bfloat16 [8192, 4096], P('blk', 'tensor'), may hold values from -0.0625 to 0.0625
- kv_weight: bfloat16 [2, 8192, 512], P(None, 'blk'), may hold values from -0.0625 to 0.0625
- out_grad: bfloat16 [10240, 4096], P('blk', 'tensor'), may hold values from -6 to 6
Outputs:
- attention: bfloat16 [10240, 4096], P('blk', 'tensor')
- grad_query_weight: bfloat16 [8192, 4096], P('blk', 'tensor')
- grad_kv_weight: bfloat16 [2, 8192, 512], P(None, 'blk')
- grad_inputs: bfloat16 [10240, 8192], P(('blk', 'tensor'))
The draws below stay inside these ranges and needn't reach their ends.
Inputs may be any that keep to these rules, and one draw needn't show every extreme that they name: `inputs`: real entries.
All inputs are finite; a program needn't handle non-finite values.
Results may differ from the reference program's by a relative error of at most 0.022.
Values may be sent and summed in bfloat16 or wider, within the bound.
A program may use at most 128 MiB of HBM per device.

```python
import math
import jax
import jax.numpy as jnp
from jax import lax

D = 8192
HD = 128
QH = 32
KVH = 4
L = 320
TOK_DEV = 320
TOKENS = 10240
N_BLK = 32
N_TENSOR = 8


def draw_inputs(key, part):
    key = jax.random.fold_in(key, 11)
    base_key, order_key = jax.random.split(key, 2)
    order = jax.random.permutation(order_key, N_BLK)
    token_block = jnp.arange(TOKENS) // TOK_DEV
    feature_block = jnp.arange(D) // (D // N_BLK)
    paired = (order[token_block][:, None] == feature_block[None, :]).astype(jnp.float32)
    boost = 1.0 + 2.0 * paired
    entries = jnp.clip(jax.random.normal(base_key, (TOKENS, D), jnp.float32), -6.0, 6.0)
    return (entries * boost).astype(jnp.bfloat16)


def levels(rng, shape, cuts, smallest, high):
    factor_of = 1.0
    for axis_at, parts in cuts:
        heights = jax.random.uniform(jax.random.fold_in(jax.random.fold_in(rng, 6), axis_at), (parts,), jnp.float32, smallest / len(cuts), high / len(cuts))
        factor_of = factor_of * jnp.repeat(jnp.exp(heights), shape[axis_at] // parts).reshape((-1,) + (1,) * (len(shape) - 1 - axis_at))
    return factor_of


def normal_values(stream_key, extent, scale, most, shards=(), kind=jnp.bfloat16):
    drawn = jax.random.normal(stream_key, extent, jnp.float32) * scale
    if len(shards) > 0:
        drawn = levels(stream_key, extent, shards, -0.22, 0.18) * drawn
    return jnp.clip(drawn, min=-most, max=most).astype(kind)


def setup_inputs(seed: int = 0) -> dict:
    seeds = jax.random.split(jax.random.key(seed), 5)
    return {
        "inputs": draw_inputs(jax.random.fold_in(seeds[4], 71), 0),
        "query_weight": normal_values(seeds[1], (D, QH * HD), D ** -0.5, 0.0625, ((0, 32), (1, 8))),
        "kv_weight": normal_values(seeds[2], (2, D, KVH * HD), D ** -0.5, 0.0625, ((1, 32),)),
        "out_grad": normal_values(seeds[3], (TOKENS, QH * HD), 1.0, 6.0, ((0, 32), (1, 8))),
    }


def rotary(states, direction):
    length = states.shape[1]
    head_width = states.shape[3]
    half_width = head_width // 2
    freq_index = jnp.arange(half_width, dtype=jnp.float32)
    frequency = jnp.exp(freq_index * (-2.0 * math.log(10000.0) / head_width))
    positions = jnp.arange(length, dtype=jnp.float32)
    angles = positions[:, None] * frequency[None, :]
    cosine = jnp.cos(angles)[None, :, None, :]
    sine_part = direction * jnp.sin(angles)[None, :, None, :]
    first_half = states[..., :half_width]
    second_half = states[..., half_width:]
    return jnp.concatenate([first_half * cosine - second_half * sine_part, second_half * cosine + first_half * sine_part], axis=-1)

def attend(query_states, key_states, value_states, grad_out, head_block):
    highest = lax.Precision.HIGHEST
    length = query_states.shape[1]
    score_scale = 1.0 / math.sqrt(query_states.shape[4])
    scores = jnp.einsum('slkgd,smkd->skglm', query_states, key_states, precision=highest) * score_scale
    row_pos = jnp.arange(length)[:, None]
    col_pos = jnp.arange(length)[None, :]
    allowed = col_pos <= row_pos
    scores = jnp.where(allowed, scores, -1e+30)
    row_max = lax.optimization_barrier(jnp.max(scores, axis=-1, keepdims=True))
    expd = jnp.exp(scores - row_max)
    row_total = lax.optimization_barrier(jnp.sum(expd, axis=-1, keepdims=True))
    probabilities = expd / row_total
    outputs = jnp.einsum('skglm,smkd->slkgd', probabilities, value_states, precision=highest)
    grad_probs = jnp.einsum('slkgd,smkd->skglm', grad_out, value_states, precision=highest)
    row_delta = jnp.einsum('slkgd,slkgd->skgl', grad_out, outputs, precision=highest)
    grad_scores = probabilities * (grad_probs - row_delta[..., None])
    grad_queries = jnp.einsum('skglm,smkd->slkgd', grad_scores, key_states, precision=highest) * score_scale
    key_heads = jnp.einsum('skglm,slkgd->smkgd', grad_scores, query_states, precision=highest) * score_scale
    value_heads = jnp.einsum('skglm,slkgd->smkgd', probabilities, grad_out, precision=highest)
    shape_now = key_heads.shape
    split_shape = (shape_now[0], shape_now[1], shape_now[2], shape_now[3] // head_block, head_block, shape_now[4])
    grad_keys = lax.optimization_barrier(jnp.sum(key_heads.reshape(split_shape), axis=4))
    grad_values = lax.optimization_barrier(jnp.sum(value_heads.reshape(split_shape), axis=4))
    return (outputs, grad_queries, grad_keys, grad_values)

def reference(inputs, query_weight, kv_weight, out_grad):
    token_count = inputs.shape[0]
    seqs_all = token_count // L
    group_size = QH // KVH
    per_rank = QH // N_TENSOR
    head_block = min(group_size, per_rank)
    kv_rank = per_rank // head_block
    block_count = QH // head_block
    query_states = jnp.dot(inputs, query_weight, preferred_element_type=jnp.float32)
    key_states = jnp.dot(inputs, kv_weight[0], preferred_element_type=jnp.float32)
    value_states = jnp.dot(inputs, kv_weight[1], preferred_element_type=jnp.float32)
    query_states = rotary(query_states.reshape(seqs_all, L, QH, HD), 1.0).reshape(seqs_all, L, KVH, group_size, HD)
    key_states = rotary(key_states.reshape(seqs_all, L, KVH, HD), 1.0)
    value_states = value_states.reshape(seqs_all, L, KVH, HD)
    grad_out = out_grad.astype(jnp.float32).reshape(seqs_all, L, KVH, group_size, HD)
    outputs, grad_queries, grad_keys, grad_values = attend(query_states, key_states, value_states, grad_out, head_block)
    attention = outputs.reshape(token_count, QH * HD).astype(jnp.bfloat16)
    grad_queries = rotary(grad_queries.reshape(seqs_all, L, QH, HD), -1.0).reshape(token_count, QH * HD).astype(jnp.bfloat16)
    grad_keys = rotary(grad_keys.reshape(seqs_all, L, block_count, HD), -1.0).reshape(token_count, block_count * HD).astype(jnp.bfloat16)
    grad_values = grad_values.reshape(token_count, block_count * HD).astype(jnp.bfloat16)
    stacked_inputs = inputs.reshape(N_BLK, TOK_DEV, D)
    stacked_queries = grad_queries.reshape(N_BLK, TOK_DEV, QH * HD)
    stacked_kv = jnp.concatenate([grad_keys, grad_values], axis=1).reshape(N_BLK, TOK_DEV, 2 * block_count * HD)

    def add_term(running, piece):
        rows_in, rows_query, rows_kv = piece
        term_query = jnp.dot(rows_in.T, rows_query, preferred_element_type=jnp.float32).astype(jnp.bfloat16)
        term_query = lax.optimization_barrier(term_query).astype(jnp.float32)
        term_kv = jnp.dot(rows_in.T, rows_kv, preferred_element_type=jnp.float32).astype(jnp.bfloat16)
        term_kv = lax.optimization_barrier(term_kv).astype(jnp.float32)
        return ((running[0] + term_query, running[1] + term_kv), None)
    start_sums = (jnp.zeros((D, QH * HD), jnp.float32), jnp.zeros((D, 2 * block_count * HD), jnp.float32))
    sums_out, unused = lax.scan(add_term, start_sums, (stacked_inputs, stacked_queries, stacked_kv))
    grad_query_weight = sums_out[0].astype(jnp.bfloat16)
    kv_blocks = sums_out[1].reshape(D, 2, KVH, block_count // KVH, HD)
    kv_heads = lax.optimization_barrier(jnp.sum(kv_blocks, axis=3)).reshape(D, 2, KVH * HD)
    grad_kv_weight = jnp.transpose(kv_heads, (1, 0, 2)).astype(jnp.bfloat16)
    grad_total = jnp.zeros((token_count, D), jnp.float32)
    for tensor_rank in range(N_TENSOR):
        q_lo = tensor_rank * per_rank * HD
        q_hi = q_lo + per_rank * HD
        b_lo = tensor_rank * kv_rank * HD
        b_hi = b_lo + kv_rank * HD
        h_lo = tensor_rank * per_rank // group_size * HD
        h_hi = h_lo + kv_rank * HD
        partial_term = jnp.dot(grad_queries[:, q_lo:q_hi], query_weight[:, q_lo:q_hi].T, preferred_element_type=jnp.float32)
        partial_term = partial_term + jnp.dot(grad_keys[:, b_lo:b_hi], kv_weight[0][:, h_lo:h_hi].T, preferred_element_type=jnp.float32)
        partial_term = partial_term + jnp.dot(grad_values[:, b_lo:b_hi], kv_weight[1][:, h_lo:h_hi].T, preferred_element_type=jnp.float32)
        partial_term = lax.optimization_barrier(partial_term.astype(jnp.bfloat16)).astype(jnp.float32)
        grad_total = grad_total + partial_term
    grad_inputs = grad_total.astype(jnp.bfloat16)
    return (attention, grad_query_weight, grad_kv_weight, grad_inputs)
```

```python
import functools
import math

import jax
import jax.numpy as jnp
import numpy as np
from jax import lax
from jax.experimental import pallas as pl
from jax.experimental.pallas import tpu as pltpu
from jax.sharding import PartitionSpec as P

HD = 128
HEADS = 4
L = 320
NZ = 8
WR = 256
WC = 640
QC = 512
AF = 128
RF = 256
MESH = pl.DeviceIdType.MESH
BF = jnp.bfloat16
F32 = jnp.float32
NT = (((1,), (1,)), ((), ()))
NN = (((1,), (0,)), ((), ()))
SCALE = 1.0 / math.sqrt(HD)
SGN = (1, -1)


def dot(a, b, dims=NN):
    return lax.dot_general(a, b, dims, preferred_element_type=F32)


def kernel(
    x_hbm, w_ref, do_ref, cos_ref, sin_ref,
    att_ref, dwq_ref, dkv_ref, dx_ref,
    xv, wg, acc, kvs, kvr, gq, gkv2, gt, qh_s, pw, rc, rz, rxf, xfs, xfr,
    dxp, ry0, ry1, keep, ls, rl, kvb,
    lsem, zs, zr, xs, xr, cs, cr, es, er,
    pcs, pcr, pxs, pxr, pzs, pzr, pfs, pfr, y0s, y0r, y1s, y1r, lls, llr, ks, kr,
):
    blk = lax.axis_index("blk")
    t = lax.axis_index("tensor")
    z, h, c = blk // 4, (blk // 2) % 2, blk % 2
    y, l = t // 2, t % 2

    def dev(zz, hh, cc, yy, ll):
        return (zz * 4 + hh * 2 + cc, yy * 2 + ll)

    znb = (dev((z + 1) % NZ, h, c, y, l), dev((z + NZ - 1) % NZ, h, c, y, l))
    ynb = (dev(z, h, c, (y + 1) % 4, l), dev(z, h, c, (y + 3) % 4, l))
    xpeer = dev(z, 1 - h, c, y, l)
    cpeer = dev(z, h, 1 - c, y, l)
    lpeer = dev(z, h, c, y, 1 - l)
    tpeers = [(blk, (t + k) % 8) for k in range(1, 8)]

    sends = []

    def send(src, dst, ssem, rsem, peer):
        copy = pltpu.make_async_remote_copy(
            src_ref=src, dst_ref=dst, send_sem=ssem, recv_sem=rsem,
            device_id=peer, device_id_type=MESH,
        )
        copy.start()
        sends.append(copy)

    def arrived(ref, ssem, rsem, peer):
        pltpu.make_async_remote_copy(
            src_ref=ref, dst_ref=ref, send_sem=ssem, recv_sem=rsem,
            device_id=peer, device_id_type=MESH,
        ).wait_recv()

    xcopy = pltpu.make_async_copy(x_hbm, xv, lsem.at[0])
    xcopy.start()
    own = h * 2 + c
    oth = (1 - h) * 2 + c
    wg[z, own] = w_ref[...]

    barrier = pltpu.get_barrier_semaphore()
    greet = [znb[0], znb[1], xpeer, cpeer] + tpeers
    for peer in greet:
        pl.semaphore_signal(barrier, inc=1, device_id=peer, device_id_type=MESH)
    pl.semaphore_wait(barrier, len(greet))

    def slot(d, k):
        return (z + 2 * NZ - SGN[k] * d) % NZ

    def own_rows(d, k):
        return pl.ds(0, WR) if d < 4 else pl.ds(k * (WR // 2), WR // 2)

    half = (WR - AF) // 2

    def oth_rows(d, k):
        if d == 0:
            return pl.ds(0, WR)
        return pl.ds(AF, WR - AF) if d < 4 else pl.ds(AF + k * half, half)

    def proj(zp):
        xcols = xv[:, pl.ds(pl.multiple_of(zp * 1024, 1024), 1024)]
        acc[...] += dot(xcols, wg[zp].reshape(4 * WR, WC))

    for k in (0, 1):
        send(wg.at[z, own], wg.at[z, own], zs.at[0, k, 1], zr.at[0, k, 1], znb[k])
    send(wg.at[z, own], wg.at[z, own], xs.at[0, 0], xr.at[0, 0], xpeer)
    send(wg.at[z, own], wg.at[z, own], cs.at[0, 0, 0], cr.at[0, 0, 0], cpeer)
    acc[...] = jnp.zeros_like(acc)
    arrived(wg.at[z, oth], xs.at[0, 0], xr.at[0, 0], xpeer)
    for k in (0, 1):
        part = wg.at[z, oth, oth_rows(1, k)]
        send(part, part, zs.at[1, k, 1], zr.at[1, k, 1], znb[k])
    send(wg.at[z, oth], wg.at[z, oth], cs.at[1, 0, 0], cr.at[1, 0, 0], cpeer)

    def tick(d, k):
        zp = slot(d, k)
        for ring, hc, rows in ((0, own, own_rows), (1, oth, oth_rows)):
            here = wg.at[zp, hc, rows(d, k)]
            arrived(here, zs.at[ring, k, d], zr.at[ring, k, d], znb[1 - k])
            if d < 4:
                part = wg.at[zp, hc, rows(d + 1, k)]
                send(part, part, zs.at[ring, k, d + 1], zr.at[ring, k, d + 1], znb[k])
            if ring == 0 and (d < 4 or k == 0):
                part = wg.at[zp, hc, pl.ds(0, AF)]
                send(part, part, xs.at[k, d], xr.at[k, d], xpeer)
            send(here, here, cs.at[ring, k, d], cr.at[ring, k, d], cpeer)

    def from_x(d, k):
        part = wg.at[slot(d, k), oth, pl.ds(0, AF)]
        arrived(part, xs.at[k, d], xr.at[k, d], xpeer)
        send(part, part, cs.at[2, k, d], cr.at[2, k, d], cpeer)

    def from_core(d, k):
        zp = slot(d, k)
        part = wg.at[zp, h * 2 + 1 - c, own_rows(d, k)]
        arrived(part, cs.at[0, k, d], cr.at[0, k, d], cpeer)
        part = wg.at[zp, (1 - h) * 2 + 1 - c, oth_rows(d, k)]
        arrived(part, cs.at[1, k, d], cr.at[1, k, d], cpeer)
        if 0 < d and (d < 4 or k == 0):
            part = wg.at[zp, (1 - h) * 2 + 1 - c, pl.ds(0, AF)]
            arrived(part, cs.at[2, k, d], cr.at[2, k, d], cpeer)

    tick(1, 0)
    tick(1, 1)
    xcopy.wait()
    from_core(0, 0)
    proj(z)
    tick(2, 0)
    tick(2, 1)
    from_x(1, 0)
    from_x(1, 1)
    for k in (0, 1):
        from_core(1, k)
        proj(slot(1, k))
    tick(3, 0)
    tick(3, 1)
    from_x(2, 0)
    from_x(2, 1)
    for k in (0, 1):
        from_core(2, k)
        proj(slot(2, k))
    tick(4, 0)
    tick(4, 1)
    from_x(3, 0)
    from_x(3, 1)
    for k in (0, 1):
        from_core(3, k)
        proj(slot(3, k))
    from_x(4, 0)
    from_core(4, 0)
    from_core(4, 1)
    proj(slot(4, 0))

    kvs[...] = acc[:, QC:]
    send(kvs, kvr, es.at[0], er.at[0], lpeer)

    cosv = cos_ref[...]
    sinv = sin_ref[...]

    def rot(v):
        return v * cosv + pltpu.roll(v, HD // 2, 1) * sinv

    def unrot(v):
        return v * cosv - pltpu.roll(v, HD // 2, 1) * sinv

    for g in range(HEADS):
        qr = rot(acc[:, pl.ds(g * HD, HD)])
        acc[:, pl.ds(g * HD, HD)] = qr * SCALE
        qh_s[g] = qr.astype(BF)

    arrived(kvr, es.at[0], er.at[0], lpeer)
    first = l == 0
    mine, other = kvs[...], kvr[...]
    kr_f = rot(jnp.where(first, mine, other))
    kh = kr_f.astype(BF)
    kl = (kr_f - kh.astype(F32)).astype(BF)
    vb = jnp.where(first, other, mine).astype(BF)
    kcat = jnp.concatenate([kh, kl, kh], axis=1)
    allowed = lax.broadcasted_iota(jnp.int32, (L, L), 1) <= lax.broadcasted_iota(
        jnp.int32, (L, L), 0
    )
    dk = jnp.zeros((L, HD), F32)
    dv = jnp.zeros((L, HD), F32)
    for g in range(HEADS):
        cols = pl.ds(g * HD, HD)
        qs = acc[:, cols]
        qsh = qs.astype(BF)
        qsl = (qs - qsh.astype(F32)).astype(BF)
        s = dot(jnp.concatenate([qsh, qsh, qsl], axis=1), kcat, NT)
        s = jnp.where(allowed, s, -1e30)
        e = jnp.exp(s - jnp.max(s, axis=1, keepdims=True))
        p = e / jnp.sum(e, axis=1, keepdims=True)
        pb = p.astype(BF)
        dob = do_ref[:, cols]
        att_ref[:, cols] = dot(pb, vb).astype(BF)
        dp = dot(dob, vb, NT)
        ds = p * (dp - jnp.sum(p * dp, axis=1, keepdims=True))
        dsb = ds.astype(BF)
        dq = unrot(dot(dsb, kh) * SCALE)
        gq[:, cols] = dq.astype(BF)
        gt[cols, :] = dq.T.astype(BF)
        dk = dk + dot(dsb.T, qh_s[g])
        dv = dv + dot(pb.T, dob)
    dk = unrot(dk * SCALE)
    gkv2[0] = jnp.where(first, dk, dv).astype(BF)
    gkv2[1] = jnp.where(first, dv, dk).astype(BF)
    send(gkv2.at[1], gkv2.at[2], es.at[1], er.at[1], lpeer)
    gt[pl.ds(QC, HD), :] = gkv2[0].astype(F32).T.astype(BF)
    arrived(gkv2.at[2], es.at[1], er.at[1], lpeer)
    gt[pl.ds(WC, HD), :] = gkv2[2].astype(F32).T.astype(BF)

    def add(dst, src, rows, n, step):
        base = 0 if rows is None else rows

        def body(i, carry):
            r = pl.ds(pl.multiple_of(base + i * step, 16), step)
            dst[r, :] = dst[r, :] + src[r, :]
            return carry

        lax.fori_loop(0, n // step, body, 0)

    def zat(o):
        return (z + NZ + o) % NZ

    def products(o):
        zp = zat(o)

        def body(j, carry):
            xcols = xv[:, pl.ds(pl.multiple_of(zp * 1024 + j * WR, WR), WR)]
            cc, hh = j % 2, j // 2
            pw[zp, cc, hh, pl.ds(0, QC), :] = dot(gt[pl.ds(0, QC), :], xcols).astype(BF)
            both = dot(gt[pl.ds(QC, HD), :], xcols) + dot(gt[pl.ds(WC, HD), :], xcols)
            pw[zp, cc, hh, pl.ds(QC, HD), :] = both.astype(BF)
            return carry

        lax.fori_loop(0, 4, body, 0)
        i = o % NZ
        send(pw.at[zp, 1 - c], rc.at[i], pcs.at[i], pcr.at[i], cpeer)

    def core_sum(o):
        zp, i = zat(o), o % NZ
        arrived(rc.at[i], pcs.at[i], pcr.at[i], cpeer)
        for hh in (0, 1):
            add(pw.at[zp, c, hh], rc.at[i, hh], None, WC, 128)
        part = pw.at[zp, c, 1 - h, pl.ds(0, RF)]
        send(part, rxf.at[i], pxs.at[i], pxr.at[i], xpeer)

    def x_sum(o):
        zp, i = zat(o), o % NZ
        arrived(rxf.at[i], pxs.at[i], pxr.at[i], xpeer)
        add(pw.at[zp, c, h], rxf.at[i], None, RF, 128)

    mid = (WC - RF) // 2

    def z_rows(s, ring, k):
        if ring == 0:
            return (0, WC) if s > 0 else (k * (WC // 2), WC // 2)
        return (RF, WC - RF) if s > 0 else (RF + k * mid, mid)

    def z_step(s, ring, k):
        hh = h if ring == 0 else 1 - h
        zp = zat(SGN[k] * (4 - s))
        if s > 0:
            base, n = z_rows(s - 1, ring, k)
            src = rz.at[s - 1, ring, k]
            arrived(
                src.at[pl.ds(base, n)], pzs.at[s - 1, ring, k], pzr.at[s - 1, ring, k],
                znb[1 - k],
            )
            add(pw.at[zp, c, hh], src, base, n, 64)
        base, n = z_rows(s, ring, k)
        send(
            pw.at[zp, c, hh, pl.ds(base, n)], rz.at[s, ring, k, pl.ds(base, n)],
            pzs.at[s, ring, k], pzr.at[s, ring, k], znb[k],
        )

    def z_last(ring):
        base, n = z_rows(3, ring, 0)
        for k in (0, 1):
            arrived(
                rz.at[3, ring, k, pl.ds(base, n)], pzs.at[3, ring, k], pzr.at[3, ring, k],
                znb[1 - k],
            )

    def dx_products(i):
        for hf in (0, 1):
            w = wg[i, 2 * hf:2 * hf + 2].reshape(2 * WR, WC)
            wkv = w[:, QC:]
            r = dot(gq[...], w[:, :QC], NT) + dot(gkv2[0], wkv, NT) + dot(gkv2[2], wkv, NT)
            dxp[i, :, hf] = r.reshape(4, 80, 512).astype(BF)
        for k in (0, 1):
            send(
                dxp.at[i, (y + 2) % 4, k], ry0.at[i, k], y0s.at[i, k], y0r.at[i, k], ynb[k]
            )

    def y_step(i):
        for k in (0, 1):
            arrived(ry0.at[i, k], y0s.at[i, k], y0r.at[i, k], ynb[1 - k])
            yy = (y + 4 + SGN[k]) % 4
            dxp[i, yy, k] = dxp[i, yy, k] + ry0[i, k]
            send(dxp.at[i, yy], ry1.at[i, k], y1s.at[i, k], y1r.at[i, k], ynb[k])

    def y_last(i):
        for k in (0, 1):
            arrived(ry1.at[i, k], y1s.at[i, k], y1r.at[i, k], ynb[1 - k])
        s = dxp[i, y].astype(F32) + ry1[i, 0].astype(F32) + ry1[i, 1].astype(F32)
        a = jnp.concatenate([s[0, :40], s[1, :40]], axis=0)
        b = jnp.concatenate([s[0, 40:], s[1, 40:]], axis=0)
        keep[i] = jnp.where(first, a, b)
        ls[i] = jnp.where(first, b, a).astype(BF)
        send(ls.at[i], rl.at[i], lls.at[i], llr.at[i], lpeer)

    def l_last(i):
        arrived(rl.at[i], lls.at[i], llr.at[i], lpeer)
        s = (keep[i] + rl[i].astype(F32)).astype(BF)
        dx_ref[:, pl.ds(i * 1024, 512)] = s[:40]
        dx_ref[:, pl.ds(i * 1024 + 512, 512)] = s[40:]

    def z_both(s, ring):
        z_step(s, ring, 0)
        z_step(s, ring, 1)

    products(4)
    products(3)
    products(-3)
    dx_products(0)
    core_sum(4)
    z_both(0, 1)
    dx_products(1)
    core_sum(3)
    core_sum(-3)
    products(2)
    products(-2)
    x_sum(4)
    z_both(0, 0)
    dx_products(2)
    dx_products(3)
    x_sum(3)
    x_sum(-3)
    core_sum(2)
    core_sum(-2)
    y_step(0)
    y_step(1)
    z_both(1, 1)
    products(1)
    products(-1)
    dx_products(4)
    z_both(1, 0)
    x_sum(2)
    x_sum(-2)
    core_sum(1)
    core_sum(-1)
    dx_products(5)
    y_step(2)
    products(0)
    dx_products(6)
    y_step(3)
    core_sum(0)
    z_both(2, 1)
    z_both(2, 0)
    dx_products(7)
    y_step(4)
    y_step(5)
    y_last(0)
    x_sum(1)
    x_sum(-1)
    x_sum(0)
    y_step(6)
    y_last(1)
    y_last(2)
    z_both(3, 1)
    z_both(3, 0)
    y_step(7)
    for i in range(3, 8):
        y_last(i)
        l_last(i - 3)

    zc = (z, c)
    z_last(1)
    for r in range(RF, WC, 128):
        rows = pl.ds(r, 128)
        xfs[pl.ds(r - RF, 128), :] = (
            pw[z, c, 1 - h, rows, :].astype(F32)
            + rz[3, 1, 0, rows, :].astype(F32)
            + rz[3, 1, 1, rows, :].astype(F32)
        ).astype(BF)
    send(xfs, xfr, pfs.at[0], pfr.at[0], xpeer)
    z_last(0)

    def total(r):
        rows = pl.ds(r, 128)
        s = (
            pw[z, c, h, rows, :].astype(F32)
            + rz[3, 0, 0, rows, :].astype(F32)
            + rz[3, 0, 1, rows, :].astype(F32)
        )
        if r >= RF:
            s = s + xfr[pl.ds(r - RF, 128), :].astype(F32)
        return s.T.astype(BF)

    for r in range(0, RF, 128):
        dwq_ref[:, pl.ds(r, 128)] = total(r)
    arrived(xfr, pfs.at[0], pfr.at[0], xpeer)
    kvb[t] = total(QC)
    for k, peer in enumerate(tpeers):
        send(kvb.at[t], kvb.at[t], ks.at[k], kr.at[t], peer)
    for r in range(RF, QC, 128):
        dwq_ref[:, pl.ds(r, 128)] = total(r)
    for i in range(5, 8):
        l_last(i)
    for k, peer in enumerate(tpeers):
        tt = (t + 1 + k) % 8
        arrived(kvb.at[tt], ks.at[k], kr.at[tt], peer)
    for yy in range(4):
        for ll in range(2):
            dkv_ref[ll, :, pl.ds(yy * HD, HD)] = kvb[yy * 2 + ll]
    for copy in sends:
        copy.wait_send()


def tables():
    i = np.arange(HD // 2, dtype=np.float64)
    ang = np.arange(L, dtype=np.float64)[:, None] * np.exp(i * (-2.0 * math.log(10000.0) / HD))
    cos, sin = np.cos(ang), np.sin(ang)
    return (
        np.concatenate([cos, cos], axis=1).astype(np.float32),
        np.concatenate([-sin, sin], axis=1).astype(np.float32),
    )


def per_device(inputs, query_weight, kv_weight, out_grad):
    t = lax.axis_index("tensor")
    kv = lax.dynamic_slice(kv_weight, (t % 2, 0, (t // 2) * HD), (1, WR, HD))[0]
    w = jnp.concatenate([query_weight, kv], axis=1)
    cos, sin = tables()
    vm = pl.BlockSpec(memory_space=pltpu.VMEM)
    dma = pltpu.SemaphoreType.DMA
    return pl.pallas_call(
        kernel,
        out_shape=(
            jax.ShapeDtypeStruct((L, QC), BF),
            jax.ShapeDtypeStruct((WR, QC), BF),
            jax.ShapeDtypeStruct((2, WR, QC), BF),
            jax.ShapeDtypeStruct((40, 8192), BF),
        ),
        in_specs=[pl.BlockSpec(memory_space=pl.ANY), vm, vm, vm, vm],
        out_specs=(vm, vm, vm, vm),
        scratch_shapes=[
            pltpu.VMEM((L, 8192), BF),
            pltpu.VMEM((NZ, 4, WR, WC), BF),
            pltpu.VMEM((L, WC), F32),
            pltpu.VMEM((L, HD), F32),
            pltpu.VMEM((L, HD), F32),
            pltpu.VMEM((L, QC), BF),
            pltpu.VMEM((3, L, HD), BF),
            pltpu.VMEM((WC + HD, L), BF),
            pltpu.VMEM((HEADS, L, HD), BF),
            pltpu.VMEM((NZ, 2, 2, WC, WR), BF),
            pltpu.VMEM((NZ, 2, WC, WR), BF),
            pltpu.VMEM((4, 2, 2, WC, WR), BF),
            pltpu.VMEM((NZ, RF, WR), BF),
            pltpu.VMEM((WC - RF, WR), BF),
            pltpu.VMEM((WC - RF, WR), BF),
            pltpu.VMEM((8, 4, 2, 80, 512), BF),
            pltpu.VMEM((8, 2, 80, 512), BF),
            pltpu.VMEM((8, 2, 2, 80, 512), BF),
            pltpu.VMEM((8, 80, 512), F32),
            pltpu.VMEM((8, 80, 512), BF),
            pltpu.VMEM((8, 80, 512), BF),
            pltpu.VMEM((8, WR, HD), BF),
            dma((1,)),
            dma((2, 2, 5)), dma((2, 2, 5)),
            dma((2, 5)), dma((2, 5)),
            dma((3, 2, 5)), dma((3, 2, 5)),
            dma((2,)), dma((2,)),
            dma((8,)), dma((8,)),
            dma((8,)), dma((8,)),
            dma((4, 2, 2)), dma((4, 2, 2)),
            dma((1,)), dma((1,)),
            dma((8, 2)), dma((8, 2)),
            dma((8, 2)), dma((8, 2)),
            dma((8,)), dma((8,)),
            dma((7,)), dma((8,)),
        ],
        compiler_params=pltpu.CompilerParams(
            collective_id=0, has_side_effects=True, vmem_limit_bytes=60 * 2**20
        ),
        cost_estimate=pl.CostEstimate(
            flops=14_000_000_000, bytes_accessed=8_000_000, transcendentals=410_000
        ),
        name="attention_step",
    )(inputs, w, out_grad, cos, sin)


def solution(mesh):
    return jax.shard_map(
        per_device,
        mesh=mesh,
        in_specs=(P("blk", None), P("blk", "tensor"), P(None, "blk", None), P("blk", "tensor")),
        out_specs=(
            P("blk", "tensor"),
            P("blk", "tensor"),
            P(None, "blk", None),
            P(("blk", "tensor"), None),
        ),
        check_vma=False,
    )
```

```python
import functools
import math

import jax
import jax.numpy as jnp
import numpy as np
from jax import lax
from jax.experimental import pallas as pl
from jax.experimental.pallas import tpu as pltpu
from jax.sharding import PartitionSpec as P

HD = 128
HEADS = 4
L = 320
NZ = 8
WR = 256
WC = 640
QC = 512
AF = 160
C1 = 384
RF = 256
MESH = pl.DeviceIdType.MESH
BF = jnp.bfloat16
F32 = jnp.float32
NT = (((1,), (1,)), ((), ()))
NN = (((1,), (0,)), ((), ()))
SCALE = 1.0 / math.sqrt(HD)
SGN = (1, -1)


PLAN = (
    ("P", 4), ("D", 0), ("P", 3), ("D", 1), ("P", -3), ("S", 4), ("Z", 0, "O", 0),
    ("Z", 0, "O", 1), ("Z", 0, "N", 0), ("Z", 0, "N", 1), ("S", 3), ("Y", 0, 0), ("Y", 0, 1),
    ("D", 2), ("P", 2), ("S", -3), ("Y", 1, 0), ("Y", 1, 1), ("D", 3), ("Z", 1, "O", 0),
    ("Z", 1, "O", 1), ("A", 4), ("Z", 0, "K", 0), ("Z", 0, "K", 1), ("Z", 0, "X", 0),
    ("Z", 0, "X", 1), ("S", 2), ("Z", 1, "N", 0), ("Z", 1, "N", 1), ("YL", 0), ("P", -2),
    ("A", 3), ("Y", 2, 0), ("Y", 2, 1), ("D", 4), ("P", 1), ("D", 5), ("Z", 2, "O", 0), ("A", -3),
    ("S", -2), ("Z", 1, "K", 0), ("Z", 1, "K", 1), ("Z", 1, "X", 0), ("Z", 1, "X", 1),
    ("Z", 2, "O", 1), ("YL", 1), ("A", 2), ("S", 1), ("Y", 3, 0), ("Y", 3, 1), ("LL", 0),
    ("P", -1), ("D", 6), ("P", 0), ("Z", 2, "N", 0), ("Z", 2, "N", 1), ("A", -2), ("YL", 2),
    ("Z", 2, "K", 1), ("S", -1), ("Y", 4, 0), ("Y", 4, 1), ("LL", 1), ("D", 7), ("Z", 2, "X", 1),
    ("A", 1), ("S", 0), ("Z", 3, "O", 0), ("Y", 5, 0), ("Y", 5, 1), ("LL", 2), ("Z", 2, "K", 0),
    ("Z", 2, "X", 0), ("Z", 3, "O", 1), ("YL", 3), ("A", -1), ("Y", 6, 0), ("Y", 6, 1), ("A", 0),
    ("Z", 3, "N", 0), ("Z", 3, "N", 1), ("LL", 3), ("YL", 4), ("Z", 3, "K", 1), ("Z", 3, "X", 1),
    ("Y", 7, 0), ("Y", 7, 1), ("Z", 3, "K", 0), ("LL", 4), ("YL", 5), ("Z", 3, "X", 0),
    ("ZL", "O"), ("YL", 6), ("LL", 5), ("ZL", "K"), ("YL", 7), ("ZL", "X"), ("ZL", "N"),
    ("LL", 6), ("LL", 7), ("FIN",),
)


def dot(a, b, dims=NN):
    return lax.dot_general(a, b, dims, preferred_element_type=F32)


def kernel(
    x_hbm, wq_hbm, kv_hbm, do_hbm, cos_hbm, sin_hbm,
    att_ref, dwq_ref, dkv_ref, dx_ref,
    do_ref, cos_ref, sin_ref, xv, wg1, wg2, acc, kvs, kvr, g1, g2, gother, gsend, gt,
    qh_s, qcat, kcat, vb_s, ds_s, dk_s, dv_s, pw, rc, rz, rxf, xfs, xfr,
    dxp, ry0, ry1, keep, ls, rl, kvb,
    lsem, zs, zr, xs, xr, cs, cr, es, er,
    pcs, pcr, pxs, pxr, pzs, pzr, pfs, pfr, y0s, y0r, y1s, y1r, lls, llr, ks, kr,
):
    blk = lax.axis_index("blk")
    t = lax.axis_index("tensor")
    z, h, c = blk // 4, (blk // 2) % 2, blk % 2
    y, l = t // 2, t % 2

    def dev(zz, hh, cc, yy, ll):
        return (zz * 4 + hh * 2 + cc, yy * 2 + ll)

    znb = (dev((z + 1) % NZ, h, c, y, l), dev((z + NZ - 1) % NZ, h, c, y, l))
    ynb = (dev(z, h, c, (y + 1) % 4, l), dev(z, h, c, (y + 3) % 4, l))
    xpeer = dev(z, 1 - h, c, y, l)
    cpeer = dev(z, h, 1 - c, y, l)
    lpeer = dev(z, h, c, y, 1 - l)
    tpeers = [(blk, (t + k) % 8) for k in range(1, 8)]

    sends = []

    def send(src, dst, ssem, rsem, peer):
        copy = pltpu.make_async_remote_copy(
            src_ref=src, dst_ref=dst, send_sem=ssem, recv_sem=rsem,
            device_id=peer, device_id_type=MESH,
        )
        copy.start()
        sends.append(copy)

    def arrived(ref, ssem, rsem, peer):
        pltpu.make_async_remote_copy(
            src_ref=ref, dst_ref=ref, send_sem=ssem, recv_sem=rsem,
            device_id=peer, device_id_type=MESH,
        ).wait_recv()

    own = h * 2 + c
    oth = (1 - h) * 2 + c
    loads = [
        pltpu.make_async_copy(src, dst, lsem.at[i])
        for i, (src, dst) in enumerate((
            (wq_hbm.at[:, pl.ds(0, C1 - HD)], wg1.at[z, own, :, pl.ds(HD, C1 - HD)]),
            (wq_hbm.at[:, pl.ds(C1 - HD, WC - C1)], wg2.at[z, own]),
            (
                kv_hbm.at[l, :, pl.ds(pl.multiple_of(y * HD, HD), HD)],
                wg1.at[z, own, :, pl.ds(0, HD)],
            ),
            (x_hbm, xv),
            (do_hbm, do_ref),
            (cos_hbm, cos_ref),
            (sin_hbm, sin_ref),
        ))
    ]
    for copy in loads:
        copy.start()

    barrier = pltpu.get_barrier_semaphore()
    greet = [znb[0], znb[1], xpeer, cpeer] + tpeers
    for peer in greet:
        pl.semaphore_signal(barrier, inc=1, device_id=peer, device_id_type=MESH)
    acc[...] = jnp.zeros_like(acc)
    for copy in loads[:3]:
        copy.wait()
    pl.semaphore_wait(barrier, len(greet))

    def slot(d, k):
        return (z + 2 * NZ - SGN[k] * d) % NZ

    piece = {"A": 0, "B": 1, "O": 2, "X": 3}
    column = {"A": own, "B": own, "O": oth, "X": oth}

    class Gather:
        def __init__(self, g, buf, split, low, width):
            self.g, self.buf, self.split = g, buf, split
            self.cols = pl.ds(low, width)

        def rows(self, p, d, k):
            f = self.split
            if p in "AX":
                return pl.ds(0, f) if f > 0 and (d < 4 or k == 0) else None
            n = WR - f
            if d < 4:
                return pl.ds(f, n)
            if p == "B" and f > 0:
                return pl.ds(f, n) if k == 1 else None
            return pl.ds(f + k * (n // 2), n // 2)

        def part(self, p, d, k):
            r = self.rows(p, d, k)
            return None if r is None else self.buf.at[slot(d, k), column[p], r]

        def z_send(self, p, d, k):
            r = self.rows(p, d, k)
            if r is not None:
                ref = self.buf.at[slot(d - 1, k), column[p], r]
                at = (self.g, piece[p], k, d)
                send(ref, ref, zs.at[at], zr.at[at], znb[k])

        def x_send(self, p, d, k, ref):
            at = (self.g, piece[p], k, d)
            send(ref, ref, xs.at[at], xr.at[at], xpeer)

        def to_core(self, p, d, k, ref):
            at = (self.g, piece[p], k, d)
            send(ref, ref, cs.at[at], cr.at[at], cpeer)

        def start(self):
            for p in "AB":
                ref = self.part(p, 0, 0)
                if ref is not None:
                    for k in (0, 1):
                        self.z_send(p, 1, k)

        def start_x(self):
            for p in "BA":
                ref = self.part(p, 0, 0)
                if ref is not None:
                    self.x_send(p, 0, 0, ref)
                    self.to_core(p, 0, 0, ref)

        def start_other(self):
            ref = self.part("O", 0, 0)
            at = (self.g, 1, 0, 0)
            arrived(ref, xs.at[at], xr.at[at], xpeer)
            for k in (0, 1):
                self.z_send("O", 1, k)
            self.to_core("O", 0, 0, ref)

        def tick(self, p, d):
            for k in (0, 1):
                ref = self.part(p, d, k)
                if ref is None:
                    continue
                at = (self.g, piece[p], k, d)
                arrived(ref, zs.at[at], zr.at[at], znb[1 - k])
                if d < 4:
                    self.z_send(p, d + 1, k)
                if p == "A":
                    self.x_send("A", d, k, ref)
                self.to_core(p, d, k, ref)

        def from_x(self, d):
            for k in (0, 1):
                ref = self.part("X", d, k)
                if ref is not None and (d > 0 or k == 0):
                    at = (self.g, 0, k, d)
                    arrived(ref, xs.at[at], xr.at[at], xpeer)
                    self.to_core("X", d, k, ref)

        def from_core(self, d, k):
            zp = slot(d, k)
            for p, hc in (("A", h * 2), ("B", h * 2), ("O", 2 - h * 2), ("X", 2 - h * 2)):
                r = self.rows(p, d, k)
                if r is not None:
                    at = (self.g, piece[p], k, d)
                    arrived(self.buf.at[zp, hc + 1 - c, r], cs.at[at], cr.at[at], cpeer)

        def proj(self, d, k):
            self.from_core(d, k)
            if d == 4:
                self.from_core(d, 1 - k)
            zp = slot(d, k)
            xcols = xv[:, pl.ds(pl.multiple_of(zp * 1024, 1024), 1024)]
            w = self.buf[zp]
            acc[:, self.cols] += dot(xcols, w.reshape(4 * WR, w.shape[-1]))

    one = Gather(0, wg1, AF, 0, C1)
    two = Gather(1, wg2, 0, C1, WC - C1)

    one.start()
    one.start_x()
    one.start_other()
    one.tick("A", 1)
    one.from_x(0)
    one.tick("B", 1)
    two.start_x()
    loads[3].wait()
    one.proj(0, 0)
    one.tick("O", 1)
    for d in (2, 3):
        one.tick("A", d)
        one.from_x(d - 1)
        one.tick("B", d)
        one.proj(d - 1, 0)
        one.tick("O", d)
        one.proj(d - 1, 1)
    two.start()
    two.start_other()
    one.tick("A", 4)
    one.from_x(3)
    one.tick("B", 4)
    one.proj(3, 0)
    one.tick("O", 4)
    one.proj(3, 1)
    two.tick("B", 1)
    two.tick("O", 1)
    one.from_x(4)
    one.proj(4, 0)

    kvs[...] = acc[:, :HD]
    send(kvs, kvr, es.at[0], er.at[0], lpeer)
    for copy in loads[4:]:
        copy.wait()
    cosv = cos_ref[...]
    sinv = sin_ref[...]

    def rot(v):
        return v * cosv + pltpu.roll(v, HD // 2, 1) * sinv

    def unrot(v):
        return v * cosv - pltpu.roll(v, HD // 2, 1) * sinv

    def queries(g):
        qr = rot(acc[:, pl.ds(HD + g * HD, HD)])
        qs = qr * SCALE
        qsh = qs.astype(BF)
        qcat[g, :, pl.ds(0, HD)] = qsh
        qcat[g, :, pl.ds(HD, HD)] = (qs - qsh.astype(F32)).astype(BF)
        qh_s[g] = qr.astype(BF)

    two.proj(0, 0)
    two.tick("B", 2)
    two.tick("O", 2)
    queries(0)
    queries(1)
    two.proj(1, 0)
    two.proj(1, 1)
    two.tick("B", 3)
    two.tick("O", 3)
    arrived(kvr, es.at[0], er.at[0], lpeer)
    first = l == 0
    kr_f = rot(jnp.where(first, kvs[...], kvr[...]))
    kh = kr_f.astype(BF)
    kcat[:, pl.ds(0, HD)] = kh
    kcat[:, pl.ds(HD, HD)] = (kr_f - kh.astype(F32)).astype(BF)
    vb_s[...] = jnp.where(first, kvr[...], kvs[...]).astype(BF)

    def head(g):
        cols = pl.ds(g * HD, HD)
        vb = vb_s[...]
        qsh, qsl = qcat[g, :, :HD], qcat[g, :, HD:]
        khv, klv = kcat[:, :HD], kcat[:, HD:]
        s = dot(
            jnp.concatenate([qsh, qsh, qsl], axis=1),
            jnp.concatenate([khv, klv, khv], axis=1), NT,
        )
        allowed = lax.broadcasted_iota(jnp.int32, (L, L), 1) <= lax.broadcasted_iota(
            jnp.int32, (L, L), 0
        )
        s = jnp.where(allowed, s, -1e30)
        e = jnp.exp(s - jnp.max(s, axis=1, keepdims=True))
        p = e / jnp.sum(e, axis=1, keepdims=True)
        pb = p.astype(BF)
        dob = do_ref[:, cols]
        att_ref[:, cols] = dot(pb, vb).astype(BF)
        dp = dot(dob, vb, NT)
        dsb = (p * (dp - jnp.sum(p * dp, axis=1, keepdims=True))).astype(BF)
        ds_s[g % 2] = dsb
        dk, dv = dot(dsb.T, qh_s[g]), dot(pb.T, dob)
        if g == 0:
            dk_s[...] = dk
            dv_s[...] = dv
        else:
            dk_s[...] += dk
            dv_s[...] += dv

    def query_grad(g):
        dq = unrot(dot(ds_s[g % 2], kcat[:, :HD]) * SCALE)
        if g < 2:
            g1[:, pl.ds(HD + g * HD, HD)] = dq.astype(BF)
        else:
            g2[:, pl.ds((g - 2) * HD, HD)] = dq.astype(BF)
        gt[pl.ds(HD + g * HD, HD), :] = dq.T.astype(BF)

    head(0)
    two.tick("B", 4)
    two.tick("O", 4)
    two.proj(2, 0)
    two.proj(2, 1)
    head(1)
    two.proj(3, 0)
    two.proj(3, 1)
    query_grad(0)
    query_grad(1)
    two.proj(4, 0)
    queries(2)
    queries(3)
    head(2)
    head(3)
    dk = unrot(dk_s[...] * SCALE)
    dv = dv_s[...]
    gsend[...] = jnp.where(first, dv, dk).astype(BF)
    send(gsend, gother, es.at[1], er.at[1], lpeer)
    mine = jnp.where(first, dk, dv)
    g1[:, pl.ds(0, HD)] = mine.astype(BF)
    gt[pl.ds(0, HD), :] = mine.T.astype(BF)
    query_grad(2)
    query_grad(3)
    arrived(gother, es.at[1], er.at[1], lpeer)
    gt[pl.ds(WC, HD), :] = gother[...].astype(F32).T.astype(BF)

    half_rest = (WC - RF) // 2
    ring_rows = {"K": (0, HD), "X": (HD, RF - HD), "O": (RF, WC - RF), "N": (RF, WC - RF)}
    order = {"K": 0, "X": 1, "O": 2, "N": 3}

    def add(dst, src, base, n, step):
        def body(i, carry):
            r = pl.ds(pl.multiple_of(base + i * step, 16), step)
            dst[r, :] = dst[r, :] + src[r, :]
            return carry

        lax.fori_loop(0, n // step, body, 0)

    def zat(o):
        return (z + NZ + o) % NZ

    def products(o):
        zp = zat(o)

        def body(j, carry):
            xcols = xv[:, pl.ds(pl.multiple_of(zp * 1024 + j * WR, WR), WR)]
            cc, hh = j % 2, j // 2
            both = dot(gt[pl.ds(0, HD), :], xcols) + dot(gt[pl.ds(WC, HD), :], xcols)
            pw[zp, cc, hh, pl.ds(0, HD), :] = both.astype(BF)
            pw[zp, cc, hh, pl.ds(HD, QC), :] = dot(gt[pl.ds(HD, QC), :], xcols).astype(BF)
            return carry

        lax.fori_loop(0, 4, body, 0)
        i = o % NZ
        send(pw.at[zp, 1 - c], rc.at[i], pcs.at[i], pcr.at[i], cpeer)

    def core_sum(o):
        zp, i = zat(o), o % NZ
        arrived(rc.at[i], pcs.at[i], pcr.at[i], cpeer)
        add(pw.at[zp, c, 1 - h], rc.at[i, 1 - h], 0, WC, 128)
        part = pw.at[zp, c, 1 - h, pl.ds(0, RF)]
        send(part, rxf.at[i], pxs.at[i], pxr.at[i], xpeer)
        add(pw.at[zp, c, h], rc.at[i, h], 0, WC, 128)

    def x_sum(o):
        zp, i = zat(o), o % NZ
        arrived(rxf.at[i], pxs.at[i], pxr.at[i], xpeer)
        add(pw.at[zp, c, h], rxf.at[i], 0, RF, 128)

    def z_rows(s, p, k):
        base, n = ring_rows[p]
        return (base, n) if s > 0 else (base + k * (n // 2), n // 2)

    def z_arrived(s, p, k):
        base, n = z_rows(s, p, k)
        ring, i = int(p == "O"), order[p]
        arrived(
            rz.at[s, ring, k, pl.ds(base, n)], pzs.at[s, i, k], pzr.at[s, i, k], znb[1 - k]
        )

    def z_step(s, p, k):
        ring, i = int(p == "O"), order[p]
        hh = 1 - h if p == "O" else h
        zp = zat(SGN[k] * (4 - s))
        if s > 0:
            z_arrived(s - 1, p, k)
            base, n = z_rows(s - 1, p, k)
            add(pw.at[zp, c, hh], rz.at[s - 1, ring, k], base, n, 64)
        base, n = z_rows(s, p, k)
        send(
            pw.at[zp, c, hh, pl.ds(base, n)], rz.at[s, ring, k, pl.ds(base, n)],
            pzs.at[s, i, k], pzr.at[s, i, k], znb[k],
        )

    def total(r, ring):
        rows = pl.ds(r, 128)
        return (
            pw[z, c, 1 - h if ring else h, rows, :].astype(F32)
            + rz[3, ring, 0, rows, :].astype(F32)
            + rz[3, ring, 1, rows, :].astype(F32)
        )

    def z_last(p):
        z_arrived(3, p, 0)
        z_arrived(3, p, 1)
        if p == "K":
            kvb[t] = total(0, 0).T.astype(BF)
            for k, peer in enumerate(tpeers):
                send(kvb.at[t], kvb.at[t], ks.at[k], kr.at[t], peer)
        if p == "X":
            for r in range(HD, RF, 128):
                dwq_ref[:, pl.ds(r - HD, 128)] = total(r, 0).T.astype(BF)
        if p == "O":
            for r in range(RF, WC, 128):
                xfs[pl.ds(r - RF, 128), :] = total(r, 1).astype(BF)
            send(xfs, xfr, pfs.at[0], pfr.at[0], xpeer)
        if p == "N":
            arrived(xfr, pfs.at[0], pfr.at[0], xpeer)
            for r in range(RF, WC, 128):
                s = total(r, 0) + xfr[pl.ds(r - RF, 128), :].astype(F32)
                dwq_ref[:, pl.ds(r - HD, 128)] = s.T.astype(BF)

    def dx_products(i):
        for hf in (0, 1):
            wa = wg1[i, 2 * hf:2 * hf + 2].reshape(2 * WR, C1)
            wb = wg2[i, 2 * hf:2 * hf + 2].reshape(2 * WR, WC - C1)
            r = dot(g1[...], wa, NT) + dot(gother[...], wa[:, :HD], NT) + dot(g2[...], wb, NT)
            dxp[i, :, hf] = r.reshape(4, 80, 512).astype(BF)
        for k in (0, 1):
            send(
                dxp.at[i, (y + 2) % 4, k], ry0.at[i, k], y0s.at[i, k], y0r.at[i, k], ynb[k]
            )

    def y_step(i, k):
        arrived(ry0.at[i, k], y0s.at[i, k], y0r.at[i, k], ynb[1 - k])
        yy = (y + 4 + SGN[k]) % 4
        dxp[i, yy, k] = dxp[i, yy, k] + ry0[i, k]
        send(dxp.at[i, yy], ry1.at[i, k], y1s.at[i, k], y1r.at[i, k], ynb[k])

    def y_last(i):
        for k in (0, 1):
            arrived(ry1.at[i, k], y1s.at[i, k], y1r.at[i, k], ynb[1 - k])
        s = dxp[i, y].astype(F32) + ry1[i, 0].astype(F32) + ry1[i, 1].astype(F32)
        a = jnp.concatenate([s[0, :40], s[1, :40]], axis=0)
        b = jnp.concatenate([s[0, 40:], s[1, 40:]], axis=0)
        keep[i] = jnp.where(first, a, b)
        ls[i] = jnp.where(first, b, a).astype(BF)
        send(ls.at[i], rl.at[i], lls.at[i], llr.at[i], lpeer)

    def l_last(i):
        arrived(rl.at[i], lls.at[i], llr.at[i], lpeer)
        s = (keep[i] + rl[i].astype(F32)).astype(BF)
        dx_ref[:, pl.ds(i * 1024, 512)] = s[:40]
        dx_ref[:, pl.ds(i * 1024 + 512, 512)] = s[40:]

    def kv_last():
        for k, peer in enumerate(tpeers):
            tt = (t + 1 + k) % 8
            arrived(kvb.at[tt], ks.at[k], kr.at[tt], peer)
        for yy in range(4):
            for ll in range(2):
                dkv_ref[ll, :, pl.ds(yy * HD, HD)] = kvb[yy * 2 + ll]

    steps = {
        "P": products, "S": core_sum, "A": x_sum, "Z": z_step, "ZL": z_last,
        "D": dx_products, "Y": y_step, "YL": y_last, "LL": l_last, "FIN": kv_last,
    }
    for name, *which in PLAN:
        steps[name](*which)
    for copy in sends:
        copy.wait_send()


def tables():
    i = np.arange(HD // 2, dtype=np.float64)
    ang = np.arange(L, dtype=np.float64)[:, None] * np.exp(i * (-2.0 * math.log(10000.0) / HD))
    cos, sin = np.cos(ang), np.sin(ang)
    return (
        np.concatenate([cos, cos], axis=1).astype(np.float32),
        np.concatenate([-sin, sin], axis=1).astype(np.float32),
    )


def place(a, b, c, d, oa, ob, oc, od, va, vb, vc, vd, sem):
    ways = ((a, va, oa), (b, vb, ob), (c, vc, oc), (d, vd, od))
    into = [pltpu.make_async_copy(src, mid, sem.at[0, i]) for i, (src, mid, _) in enumerate(ways)]
    out = [pltpu.make_async_copy(mid, dst, sem.at[1, i]) for i, (_, mid, dst) in enumerate(ways)]
    for copy in into:
        copy.start()
    for first, second in zip(into, out):
        first.wait()
        second.start()
    for copy in out:
        copy.wait()


def per_device(inputs, query_weight, kv_weight, out_grad):
    cos, sin = tables()
    vm = pl.BlockSpec(memory_space=pltpu.VMEM)
    anywhere = pl.BlockSpec(memory_space=pl.ANY)
    dma = pltpu.SemaphoreType.DMA
    shapes = (
        jax.ShapeDtypeStruct((L, QC), BF),
        jax.ShapeDtypeStruct((WR, QC), BF),
        jax.ShapeDtypeStruct((2, WR, QC), BF),
        jax.ShapeDtypeStruct((40, 8192), BF),
    )
    results = pl.pallas_call(
        kernel,
        out_shape=shapes,
        in_specs=[anywhere] * 6,
        out_specs=(vm, vm, vm, vm),
        scratch_shapes=[
            pltpu.VMEM((L, QC), BF),
            pltpu.VMEM((L, HD), F32),
            pltpu.VMEM((L, HD), F32),
            pltpu.VMEM((L, 8192), BF),
            pltpu.VMEM((NZ, 4, WR, C1), BF),
            pltpu.VMEM((NZ, 4, WR, WC - C1), BF),
            pltpu.VMEM((L, WC), F32),
            pltpu.VMEM((L, HD), F32),
            pltpu.VMEM((L, HD), F32),
            pltpu.VMEM((L, C1), BF),
            pltpu.VMEM((L, WC - C1), BF),
            pltpu.VMEM((L, HD), BF),
            pltpu.VMEM((L, HD), BF),
            pltpu.VMEM((WC + HD, L), BF),
            pltpu.VMEM((HEADS, L, HD), BF),
            pltpu.VMEM((HEADS, L, 2 * HD), BF),
            pltpu.VMEM((L, 2 * HD), BF),
            pltpu.VMEM((L, HD), BF),
            pltpu.VMEM((2, L, L), BF),
            pltpu.VMEM((L, HD), F32),
            pltpu.VMEM((L, HD), F32),
            pltpu.VMEM((NZ, 2, 2, WC, WR), BF),
            pltpu.VMEM((NZ, 2, WC, WR), BF),
            pltpu.VMEM((4, 2, 2, WC, WR), BF),
            pltpu.VMEM((NZ, RF, WR), BF),
            pltpu.VMEM((WC - RF, WR), BF),
            pltpu.VMEM((WC - RF, WR), BF),
            pltpu.VMEM((8, 4, 2, 80, 512), BF),
            pltpu.VMEM((8, 2, 80, 512), BF),
            pltpu.VMEM((8, 2, 2, 80, 512), BF),
            pltpu.VMEM((8, 80, 512), F32),
            pltpu.VMEM((8, 80, 512), BF),
            pltpu.VMEM((8, 80, 512), BF),
            pltpu.VMEM((8, WR, HD), BF),
            dma((7,)),
            dma((2, 3, 2, 5)), dma((2, 3, 2, 5)),
            dma((2, 2, 2, 5)), dma((2, 2, 2, 5)),
            dma((2, 4, 2, 5)), dma((2, 4, 2, 5)),
            dma((2,)), dma((2,)),
            dma((8,)), dma((8,)),
            dma((8,)), dma((8,)),
            dma((4, 4, 2)), dma((4, 4, 2)),
            dma((1,)), dma((1,)),
            dma((8, 2)), dma((8, 2)),
            dma((8, 2)), dma((8, 2)),
            dma((8,)), dma((8,)),
            dma((7,)), dma((8,)),
        ],
        compiler_params=pltpu.CompilerParams(
            collective_id=0, has_side_effects=True, vmem_limit_bytes=60 * 2**20
        ),
        cost_estimate=pl.CostEstimate(
            flops=14_000_000_000, bytes_accessed=8_000_000, transcendentals=410_000
        ),
        name="attention_step",
    )(inputs, query_weight, kv_weight, out_grad, cos, sin)
    return pl.pallas_call(
        place,
        out_shape=shapes,
        in_specs=[anywhere] * 4,
        out_specs=(anywhere,) * 4,
        scratch_shapes=[pltpu.VMEM(s.shape, s.dtype) for s in shapes] + [dma((2, 4))],
        name="place",
    )(*results)


def solution(mesh):
    return jax.shard_map(
        per_device,
        mesh=mesh,
        in_specs=(P("blk", None), P("blk", "tensor"), P(None, "blk", None), P("blk", "tensor")),
        out_specs=(
            P("blk", "tensor"),
            P("blk", "tensor"),
            P(None, "blk", None),
            P(("blk", "tensor"), None),
        ),
        check_vma=False,
    )
```

```python
import functools
import math

import jax
import jax.numpy as jnp
import numpy as np
from jax import lax
from jax.experimental import pallas as pl
from jax.experimental.pallas import tpu as pltpu
from jax.sharding import PartitionSpec as P

HD = 128
HEADS = 4
L = 320
NZ = 8
WR = 256
WC = 640
QC = 512
AF = 160
C1 = 384
DIRECT = 6
MESH = pl.DeviceIdType.MESH
BF = jnp.bfloat16
F32 = jnp.float32
NT = (((1,), (1,)), ((), ()))
NN = (((1,), (0,)), ((), ()))
SCALE = 1.0 / math.sqrt(HD)
SGN = (1, -1)


PLAN = (
    ("P", 1, 4), ("PR", 2), ("T4",), ("PR", 3), ("P", 1, 0), ("P", 1, -3), ("S", 1, 4),
    ("Z", 0, "N", 1), ("PR", 4), ("H", 2), ("H", 3), ("HS",), ("Z", 0, "O", 0), ("Z", 0, "O", 1),
    ("P", 1, 1), ("P", 1, 3), ("P", 1, 2), ("Z", 0, "N", 0), ("S", 1, -3), ("QG", 2), ("QG", 3),
    ("P", 1, -2), ("Z", 1, "N", 1), ("S", 1, 3), ("Z", 1, "O", 0), ("KV",), ("D", 7), ("D", 3),
    ("P", 2, 4), ("Z", 1, "N", 0), ("D", 4), ("D", 5), ("P", 2, 3), ("S", 2, 4), ("Z", 0, "M", 0),
    ("Z", 0, "Q", 1), ("Z", 1, "O", 1), ("Y", 3, 1), ("Y", 3, 0), ("Z", 0, "Q", 0), ("P", 2, -3),
    ("P", 2, -1), ("Z", 0, "M", 1), ("P", 2, 2), ("S", 2, 3), ("Y", 4, 1), ("P", 2, -2),
    ("Y", 4, 0), ("S", 2, -3), ("Z", 1, "M", 0), ("Z", 1, "Q", 1), ("S", 2, -1), ("D", 2),
    ("A", 2, 4), ("Z", 0, "K", 0), ("Z", 0, "K", 1), ("Y", 5, 0), ("S", 2, -2), ("Y", 5, 1),
    ("Z", 1, "Q", 0), ("Z", 1, "M", 1), ("S", 2, 2), ("P", 2, 1), ("D", 6), ("Z", 2, "M", 0),
    ("Z", 2, "Q", 1), ("D", 1), ("A", 2, 3), ("A", 2, -3), ("Z", 1, "K", 0), ("S", 2, 1),
    ("Z", 1, "K", 1), ("S", 1, -2), ("Y", 2, 0), ("Y", 2, 1), ("A", 2, -1), ("P", 2, 0),
    ("Z", 2, "O", 1), ("Z", 2, "Q", 0), ("A", 2, -2), ("D", 0), ("S", 1, 2), ("Z", 2, "M", 1),
    ("Z", 2, "O", 0), ("YL", 5), ("YL", 4), ("Y", 1, 0), ("Y", 1, 1), ("LQ", 7), ("YL", 3),
    ("S", 2, 0), ("A", 2, 2), ("Z", 2, "K", 1), ("Z", 2, "K", 0), ("P", 1, -1), ("Z", 3, "Q", 1),
    ("YL", 2), ("Z", 3, "Q", 0), ("Z", 2, "N", 0), ("LQ", 6), ("S", 1, 0), ("A", 2, 1),
    ("Y", 0, 0), ("Z", 2, "N", 1), ("Y", 0, 1), ("S", 1, -1), ("Z", 3, "K", 0), ("Z", 3, "K", 1),
    ("Z", 3, "O", 1), ("YL", 1), ("Z", 3, "M", 1), ("YQ", 7, 1), ("S", 1, 1), ("YQ", 6, 1),
    ("ZL", "Q"), ("YQ", 6, 0), ("Z", 3, "O", 0), ("Z", 3, "M", 0), ("A", 2, 0), ("YQ", 7, 0),
    ("YL", 0), ("Z", 3, "N", 1), ("Z", 3, "N", 0), ("ZL", "K"), ("ZL", "O"), ("LL", 1), ("LL", 4),
    ("LL", 3), ("LL", 0), ("LL", 2), ("FQ", 6), ("ZL", "M"), ("FQ", 7), ("FIN",), ("LL", 5),
    ("ZL", "N"),
)


def dot(a, b, dims=NN):
    return lax.dot_general(a, b, dims, preferred_element_type=F32)


def kernel(
    x_hbm, wq_hbm, kv_hbm, do_hbm, cos_hbm, sin_hbm,
    att_ref, dwq_ref, dkv_ref, dx_ref,
    do_ref, cos_ref, sin_ref, xv, wg1, wg2, acc, kvs, kvr, g1, g2, gother, gsend, gt,
    qh_s, qcat, kcat, vb_s, ds_s, dk_s, dv_s, pw, rc, rz, rxf, xfs, xfr,
    dxp, ry0, ry1, keep, ls, rl, dxq, rlq, ry0q, ry1q, kvb,
    lsem, zs, zr, xs, xr, cs, cr, es, er,
    pcs, pcr, pxs, pxr, pzs, pzr, pfs, pfr, y0s, y0r, y1s, y1r, lls, llr, ks, kr,
):
    blk = lax.axis_index("blk")
    t = lax.axis_index("tensor")
    z, h, c = blk // 4, (blk // 2) % 2, blk % 2
    y, l = t // 2, t % 2

    def dev(zz, hh, cc, yy, ll):
        return (zz * 4 + hh * 2 + cc, yy * 2 + ll)

    znb = (dev((z + 1) % NZ, h, c, y, l), dev((z + NZ - 1) % NZ, h, c, y, l))
    ynb = (dev(z, h, c, (y + 1) % 4, l), dev(z, h, c, (y + 3) % 4, l))
    xpeer = dev(z, 1 - h, c, y, l)
    cpeer = dev(z, h, 1 - c, y, l)
    lpeer = dev(z, h, c, y, 1 - l)
    tpeers = [(blk, (t + k) % 8) for k in range(1, 8)]

    sends = []

    def send(src, dst, ssem, rsem, peer):
        copy = pltpu.make_async_remote_copy(
            src_ref=src, dst_ref=dst, send_sem=ssem, recv_sem=rsem,
            device_id=peer, device_id_type=MESH,
        )
        copy.start()
        sends.append(copy)

    def arrived(ref, ssem, rsem, peer):
        pltpu.make_async_remote_copy(
            src_ref=ref, dst_ref=ref, send_sem=ssem, recv_sem=rsem,
            device_id=peer, device_id_type=MESH,
        ).wait_recv()

    own = h * 2 + c
    oth = (1 - h) * 2 + c
    loads = [
        pltpu.make_async_copy(src, dst, lsem.at[i])
        for i, (src, dst) in enumerate((
            (wq_hbm.at[:, pl.ds(0, C1 - HD)], wg1.at[z, own, :, pl.ds(HD, C1 - HD)]),
            (wq_hbm.at[:, pl.ds(C1 - HD, WC - C1)], wg2.at[z, own]),
            (
                kv_hbm.at[l, :, pl.ds(pl.multiple_of(y * HD, HD), HD)],
                wg1.at[z, own, :, pl.ds(0, HD)],
            ),
            (x_hbm, xv),
            (do_hbm, do_ref),
            (cos_hbm, cos_ref),
            (sin_hbm, sin_ref),
        ))
    ]
    for copy in loads:
        copy.start()

    barrier = pltpu.get_barrier_semaphore()
    greet = [znb[0], znb[1], xpeer, cpeer] + tpeers
    for peer in greet:
        pl.semaphore_signal(barrier, inc=1, device_id=peer, device_id_type=MESH)
    acc[...] = jnp.zeros_like(acc)
    for copy in loads[:3]:
        copy.wait()
    pl.semaphore_wait(barrier, len(greet))

    def slot(d, k):
        return (z + 2 * NZ - SGN[k] * d) % NZ

    piece = {"A": 0, "B": 1, "O": 2, "X": 3}
    column = {"A": own, "B": own, "O": oth, "X": oth}

    class Gather:
        def __init__(self, g, buf, split, low, width):
            self.g, self.buf, self.split = g, buf, split
            self.cols = pl.ds(low, width)

        def rows(self, p, d, k):
            f = self.split
            if p in "AX":
                return pl.ds(0, f) if f > 0 and (d < 4 or k == 0) else None
            n = WR - f
            if d < 4:
                return pl.ds(f, n)
            if p == "B" and f > 0:
                return pl.ds(f, n) if k == 1 else None
            return pl.ds(f + k * (n // 2), n // 2)

        def part(self, p, d, k):
            r = self.rows(p, d, k)
            return None if r is None else self.buf.at[slot(d, k), column[p], r]

        def z_send(self, p, d, k):
            r = self.rows(p, d, k)
            if r is not None:
                ref = self.buf.at[slot(d - 1, k), column[p], r]
                at = (self.g, piece[p], k, d)
                send(ref, ref, zs.at[at], zr.at[at], znb[k])

        def x_send(self, p, d, k, ref):
            at = (self.g, piece[p], k, d)
            send(ref, ref, xs.at[at], xr.at[at], xpeer)

        def to_core(self, p, d, k, ref):
            at = (self.g, piece[p], k, d)
            send(ref, ref, cs.at[at], cr.at[at], cpeer)

        def start(self):
            for p in "AB":
                ref = self.part(p, 0, 0)
                if ref is not None:
                    for k in (0, 1):
                        self.z_send(p, 1, k)

        def start_x(self):
            for p in "BA":
                ref = self.part(p, 0, 0)
                if ref is not None:
                    self.x_send(p, 0, 0, ref)
                    self.to_core(p, 0, 0, ref)

        def start_other(self):
            ref = self.part("O", 0, 0)
            at = (self.g, 1, 0, 0)
            arrived(ref, xs.at[at], xr.at[at], xpeer)
            for k in (0, 1):
                self.z_send("O", 1, k)
            self.to_core("O", 0, 0, ref)

        def tick(self, p, d):
            for k in (0, 1):
                ref = self.part(p, d, k)
                if ref is None:
                    continue
                at = (self.g, piece[p], k, d)
                arrived(ref, zs.at[at], zr.at[at], znb[1 - k])
                if d < 4:
                    self.z_send(p, d + 1, k)
                if p == "A":
                    self.x_send("A", d, k, ref)
                self.to_core(p, d, k, ref)

        def from_x(self, d):
            for k in (0, 1):
                ref = self.part("X", d, k)
                if ref is not None and (d > 0 or k == 0):
                    at = (self.g, 0, k, d)
                    arrived(ref, xs.at[at], xr.at[at], xpeer)
                    self.to_core("X", d, k, ref)

        def from_core(self, d, k):
            zp = slot(d, k)
            for p, hc in (("A", h * 2), ("B", h * 2), ("O", 2 - h * 2), ("X", 2 - h * 2)):
                r = self.rows(p, d, k)
                if r is not None:
                    at = (self.g, piece[p], k, d)
                    arrived(self.buf.at[zp, hc + 1 - c, r], cs.at[at], cr.at[at], cpeer)

        def proj(self, d, k):
            self.from_core(d, k)
            if d == 4:
                self.from_core(d, 1 - k)
            zp = slot(d, k)
            xcols = xv[:, pl.ds(pl.multiple_of(zp * 1024, 1024), 1024)]
            w = self.buf[zp]
            acc[:, self.cols] += dot(xcols, w.reshape(4 * WR, w.shape[-1]))

    one = Gather(0, wg1, AF, 0, C1)
    two = Gather(1, wg2, 0, C1, WC - C1)

    one.start()
    one.start_x()
    one.start_other()
    one.tick("A", 1)
    one.from_x(0)
    one.tick("B", 1)
    two.start_x()
    loads[3].wait()
    one.proj(0, 0)
    one.tick("O", 1)
    for d in (2, 3):
        one.tick("A", d)
        one.from_x(d - 1)
        one.tick("B", d)
        one.proj(d - 1, 0)
        one.tick("O", d)
        one.proj(d - 1, 1)
    two.start()
    two.start_other()
    one.tick("A", 4)
    one.from_x(3)
    one.tick("B", 4)
    one.proj(3, 0)
    one.tick("O", 4)
    one.proj(3, 1)
    two.tick("B", 1)
    two.tick("O", 1)
    one.from_x(4)
    one.proj(4, 0)

    kvs[...] = acc[:, :HD]
    send(kvs, kvr, es.at[0], er.at[0], lpeer)
    for copy in loads[4:]:
        copy.wait()
    cosv = cos_ref[...]
    sinv = sin_ref[...]

    def rot(v):
        return v * cosv + pltpu.roll(v, HD // 2, 1) * sinv

    def unrot(v):
        return v * cosv - pltpu.roll(v, HD // 2, 1) * sinv

    def queries(g):
        qr = rot(acc[:, pl.ds(HD + g * HD, HD)])
        qs = qr * SCALE
        qsh = qs.astype(BF)
        qcat[g, :, pl.ds(0, HD)] = qsh
        qcat[g, :, pl.ds(HD, HD)] = (qs - qsh.astype(F32)).astype(BF)
        qh_s[g] = qr.astype(BF)

    two.proj(0, 0)
    two.tick("B", 2)
    two.tick("O", 2)
    queries(0)
    queries(1)
    two.proj(1, 0)
    two.proj(1, 1)
    two.tick("B", 3)
    two.tick("O", 3)
    arrived(kvr, es.at[0], er.at[0], lpeer)
    first = l == 0
    kr_f = rot(jnp.where(first, kvs[...], kvr[...]))
    kh = kr_f.astype(BF)
    kcat[:, pl.ds(0, HD)] = kh
    kcat[:, pl.ds(HD, HD)] = (kr_f - kh.astype(F32)).astype(BF)
    vb_s[...] = jnp.where(first, kvr[...], kvs[...]).astype(BF)

    def head(g):
        cols = pl.ds(g * HD, HD)
        vb = vb_s[...]
        qsh, qsl = qcat[g, :, :HD], qcat[g, :, HD:]
        khv, klv = kcat[:, :HD], kcat[:, HD:]
        s = dot(
            jnp.concatenate([qsh, qsh, qsl], axis=1),
            jnp.concatenate([khv, klv, khv], axis=1), NT,
        )
        allowed = lax.broadcasted_iota(jnp.int32, (L, L), 1) <= lax.broadcasted_iota(
            jnp.int32, (L, L), 0
        )
        s = jnp.where(allowed, s, -1e30)
        e = jnp.exp(s - jnp.max(s, axis=1, keepdims=True))
        p = e / jnp.sum(e, axis=1, keepdims=True)
        pb = p.astype(BF)
        dob = do_ref[:, cols]
        att_ref[:, cols] = dot(pb, vb).astype(BF)
        dp = dot(dob, vb, NT)
        dsb = (p * (dp - jnp.sum(p * dp, axis=1, keepdims=True))).astype(BF)
        ds_s[g % 2] = dsb
        dk, dv = dot(dsb.T, qh_s[g]), dot(pb.T, dob)
        if g == 0:
            dk_s[...] = dk
            dv_s[...] = dv
        else:
            dk_s[...] += dk
            dv_s[...] += dv

    def query_grad(g):
        dq = unrot(dot(ds_s[g % 2], kcat[:, :HD]) * SCALE)
        if g < 2:
            g1[:, pl.ds(HD + g * HD, HD)] = dq.astype(BF)
        else:
            g2[:, pl.ds((g - 2) * HD, HD)] = dq.astype(BF)
        gt[pl.ds((g if g < 2 else g + 1) * HD, HD), :] = dq.T.astype(BF)

    head(0)
    head(1)
    query_grad(0)
    query_grad(1)

    def last_tick():
        two.tick("B", 4)
        two.tick("O", 4)

    def projections(d):
        two.proj(d, 0)
        if d < 4:
            two.proj(d, 1)
        else:
            queries(2)
            queries(3)

    def send_kv_grad():
        dk, dv = unrot(dk_s[...] * SCALE), dv_s[...]
        gsend[...] = jnp.where(first, dv, dk).astype(BF)
        send(gsend, gother, es.at[1], er.at[1], lpeer)
        mine = jnp.where(first, dk, dv)
        g1[:, pl.ds(0, HD)] = mine.astype(BF)
        gt[pl.ds(2 * HD, HD), :] = mine.T.astype(BF)

    def kv_grad():
        arrived(gother, es.at[1], er.at[1], lpeer)
        gt[pl.ds(WC, HD), :] = gother[...].astype(F32).T.astype(BF)

    pieces = {
        "N": (0, 0, 2 * HD), "O": (1, 0, 2 * HD),
        "K": (0, 2 * HD, HD), "M": (0, 3 * HD, 2 * HD), "Q": (1, 3 * HD, 2 * HD),
    }
    order = {p: i for i, p in enumerate(pieces)}
    group_rows = {1: (0, 2 * HD), 2: (2 * HD, 3 * HD)}

    def add(dst, src, base, n, step, shift=0):
        def body(i, carry):
            at = pl.multiple_of(base + i * step, 16)
            r = pl.ds(at, step)
            dst[r, :] = dst[r, :] + src[pl.ds(pl.multiple_of(at - shift, 16), step), :]
            return carry

        lax.fori_loop(0, n // step, body, 0)

    def zat(o):
        return (z + NZ + o) % NZ

    def products(g, o):
        zp = zat(o)

        def body(j, carry):
            xcols = xv[:, pl.ds(pl.multiple_of(zp * 1024 + j * WR, WR), WR)]
            cc, hh = j % 2, j // 2
            if g == 1:
                pw[zp, cc, hh, pl.ds(0, 256), :] = dot(gt[pl.ds(0, 256), :], xcols).astype(BF)
            else:
                both = dot(gt[pl.ds(256, HD), :], xcols) + dot(gt[pl.ds(WC, HD), :], xcols)
                pw[zp, cc, hh, pl.ds(256, HD), :] = both.astype(BF)
                pw[zp, cc, hh, pl.ds(384, 256), :] = dot(
                    gt[pl.ds(384, 256), :], xcols
                ).astype(BF)
            return carry

        lax.fori_loop(0, 4, body, 0)
        i = o % NZ
        r = pl.ds(*group_rows[g])
        at = (g - 1, i)
        send(pw.at[zp, 1 - c, :, r], rc.at[i, :, r], pcs.at[at], pcr.at[at], cpeer)

    def core_sum(g, o):
        zp, i = zat(o), o % NZ
        low, n = group_rows[g]
        r = pl.ds(low, n)
        at = (g - 1, i)
        arrived(rc.at[i, :, r], pcs.at[at], pcr.at[at], cpeer)
        add(pw.at[zp, c, 1 - h], rc.at[i, 1 - h], low, n, 128)
        if g == 2:
            part = pw.at[zp, c, 1 - h, pl.ds(low, HD)]
            send(part, rxf.at[i], pxs.at[i], pxr.at[i], xpeer)
        add(pw.at[zp, c, h], rc.at[i, h], low, n, 128)

    def x_sum(g, o):
        zp, i = zat(o), o % NZ
        arrived(rxf.at[i], pxs.at[i], pxr.at[i], xpeer)
        low = group_rows[g][0]
        add(pw.at[zp, c, h], rxf.at[i], low, HD, 128, low)

    def z_rows(s, p, k):
        base, n = pieces[p][1:]
        return (base, n) if s > 0 else (base + k * (n // 2), n // 2)

    def z_arrived(s, p, k):
        base, n = z_rows(s, p, k)
        ring, i = pieces[p][0], order[p]
        arrived(
            rz.at[s, ring, k, pl.ds(base, n)], pzs.at[s, i, k], pzr.at[s, i, k], znb[1 - k]
        )

    def z_step(s, p, k):
        ring, i = pieces[p][0], order[p]
        hh = 1 - h if ring else h
        zp = zat(SGN[k] * (4 - s))
        if s > 0:
            z_arrived(s - 1, p, k)
            base, n = z_rows(s - 1, p, k)
            add(pw.at[zp, c, hh], rz.at[s - 1, ring, k], base, n, 64)
        base, n = z_rows(s, p, k)
        send(
            pw.at[zp, c, hh, pl.ds(base, n)], rz.at[s, ring, k, pl.ds(base, n)],
            pzs.at[s, i, k], pzr.at[s, i, k], znb[k],
        )

    def total(r, ring):
        rows = pl.ds(r, 128)
        return (
            pw[z, c, 1 - h if ring else h, rows, :].astype(F32)
            + rz[3, ring, 0, rows, :].astype(F32)
            + rz[3, ring, 1, rows, :].astype(F32)
        )

    last = {"O": (0, 0), "N": (0, 0), "Q": (1, 2 * HD), "M": (1, 2 * HD)}

    def z_last(p):
        z_arrived(3, p, 0)
        z_arrived(3, p, 1)
        ring, base, n = pieces[p]
        if p == "K":
            kvb[t] = total(base, 0).T.astype(BF)
            for k, peer in enumerate(tpeers):
                send(kvb.at[t], kvb.at[t], ks.at[k], kr.at[t], peer)
            return
        if p in last:
            i, at = last[p]
        if p in "OQ":
            for r in range(0, n, 128):
                xfs[pl.ds(at + r, 128), :] = total(base + r, 1).astype(BF)
            rows = pl.ds(at, n)
            send(xfs.at[rows], xfr.at[rows], pfs.at[i], pfr.at[i], xpeer)
            return
        if p in "NM":
            arrived(xfr.at[pl.ds(at, n)], pfs.at[i], pfr.at[i], xpeer)
        for r in range(0, n, 128):
            s = total(base + r, 0)
            if p in "NM":
                s = s + xfr[pl.ds(at + r, 128), :].astype(F32)
            low = base + r if base < 256 else base + r - HD
            dwq_ref[:, pl.ds(low, 128)] = s.T.astype(BF)

    def dx_products(i):
        halves = []
        for hf in (0, 1):
            wa = wg1[i, 2 * hf:2 * hf + 2].reshape(2 * WR, C1)
            wb = wg2[i, 2 * hf:2 * hf + 2].reshape(2 * WR, WC - C1)
            r = dot(g1[...], wa, NT) + dot(gother[...], wa[:, :HD], NT) + dot(g2[...], wb, NT)
            if i < DIRECT:
                dxp[i, :, hf] = r.reshape(4, 80, 512).astype(BF)
            else:
                halves.append(r.reshape(4, 2, 40, 512))
        if i < DIRECT:
            for k in (0, 1):
                send(
                    dxp.at[i, (y + 2) % 4, k], ry0.at[i, k], y0s.at[i, k], y0r.at[i, k],
                    ynb[k],
                )
            return
        j = i - DIRECT
        for ll in (0, 1):
            both = jnp.concatenate([halves[0][:, ll], halves[1][:, ll]], axis=1)
            dxq[j, ll] = both.astype(BF)
        send(dxq.at[j, 1 - l], rlq.at[j], lls.at[i], llr.at[i], lpeer)

    def lq_step(i):
        j = i - DIRECT
        arrived(rlq.at[j], lls.at[i], llr.at[i], lpeer)
        dxq[j, l] = dxq[j, l] + rlq[j]
        for k in (0, 1):
            send(
                dxq.at[j, l, (y + 2) % 4, :, pl.ds(k * 256, 256)], ry0q.at[j, k],
                y0s.at[i, k], y0r.at[i, k], ynb[k],
            )

    def yq_step(i, k):
        j = i - DIRECT
        arrived(ry0q.at[j, k], y0s.at[i, k], y0r.at[i, k], ynb[1 - k])
        yy = (y + 4 + SGN[k]) % 4
        lanes = pl.ds(k * 256, 256)
        dxq[j, l, yy, :, lanes] = dxq[j, l, yy, :, lanes] + ry0q[j, k]
        send(dxq.at[j, l, yy], ry1q.at[j, k], y1s.at[i, k], y1r.at[i, k], ynb[k])

    def yq_last(i):
        j = i - DIRECT
        for k in (0, 1):
            arrived(ry1q.at[j, k], y1s.at[i, k], y1r.at[i, k], ynb[1 - k])
        s = dxq[j, l, y].astype(F32) + ry1q[j, 0].astype(F32) + ry1q[j, 1].astype(F32)
        dx_ref[:, pl.ds(i * 1024, 512)] = s[:40].astype(BF)
        dx_ref[:, pl.ds(i * 1024 + 512, 512)] = s[40:].astype(BF)

    def y_step(i, k):
        arrived(ry0.at[i, k], y0s.at[i, k], y0r.at[i, k], ynb[1 - k])
        yy = (y + 4 + SGN[k]) % 4
        dxp[i, yy, k] = dxp[i, yy, k] + ry0[i, k]
        send(dxp.at[i, yy], ry1.at[i, k], y1s.at[i, k], y1r.at[i, k], ynb[k])

    def y_last(i):
        for k in (0, 1):
            arrived(ry1.at[i, k], y1s.at[i, k], y1r.at[i, k], ynb[1 - k])
        s = dxp[i, y].astype(F32) + ry1[i, 0].astype(F32) + ry1[i, 1].astype(F32)
        a = jnp.concatenate([s[0, :40], s[1, :40]], axis=0)
        b = jnp.concatenate([s[0, 40:], s[1, 40:]], axis=0)
        keep[i] = jnp.where(first, a, b)
        ls[i] = jnp.where(first, b, a).astype(BF)
        send(ls.at[i], rl.at[i], lls.at[i], llr.at[i], lpeer)

    def l_last(i):
        arrived(rl.at[i], lls.at[i], llr.at[i], lpeer)
        s = (keep[i] + rl[i].astype(F32)).astype(BF)
        dx_ref[:, pl.ds(i * 1024, 512)] = s[:40]
        dx_ref[:, pl.ds(i * 1024 + 512, 512)] = s[40:]

    def kv_last():
        for k, peer in enumerate(tpeers):
            tt = (t + 1 + k) % 8
            arrived(kvb.at[tt], ks.at[k], kr.at[tt], peer)
        for yy in range(4):
            for ll in range(2):
                dkv_ref[ll, :, pl.ds(yy * HD, HD)] = kvb[yy * 2 + ll]

    steps = {
        "P": products, "S": core_sum, "A": x_sum, "Z": z_step, "ZL": z_last,
        "D": dx_products, "Y": y_step, "YL": y_last, "LL": l_last, "FIN": kv_last,
        "LQ": lq_step, "YQ": yq_step, "FQ": yq_last, "T4": last_tick, "PR": projections,
        "H": head, "HS": send_kv_grad, "QG": query_grad, "KV": kv_grad,
    }
    for name, *which in PLAN:
        steps[name](*which)
    for copy in sends:
        copy.wait_send()


def tables():
    i = np.arange(HD // 2, dtype=np.float64)
    ang = np.arange(L, dtype=np.float64)[:, None] * np.exp(i * (-2.0 * math.log(10000.0) / HD))
    cos, sin = np.cos(ang), np.sin(ang)
    return (
        np.concatenate([cos, cos], axis=1).astype(np.float32),
        np.concatenate([-sin, sin], axis=1).astype(np.float32),
    )


def place(a, b, c, d, oa, ob, oc, od, va, vb, vc, vd, sem):
    ways = ((a, va, oa), (b, vb, ob), (c, vc, oc), (d, vd, od))
    into = [pltpu.make_async_copy(src, mid, sem.at[0, i]) for i, (src, mid, _) in enumerate(ways)]
    out = [pltpu.make_async_copy(mid, dst, sem.at[1, i]) for i, (_, mid, dst) in enumerate(ways)]
    for copy in into:
        copy.start()
    for first, second in zip(into, out):
        first.wait()
        second.start()
    for copy in out:
        copy.wait()


def per_device(inputs, query_weight, kv_weight, out_grad):
    cos, sin = tables()
    vm = pl.BlockSpec(memory_space=pltpu.VMEM)
    anywhere = pl.BlockSpec(memory_space=pl.ANY)
    dma = pltpu.SemaphoreType.DMA
    shapes = (
        jax.ShapeDtypeStruct((L, QC), BF),
        jax.ShapeDtypeStruct((WR, QC), BF),
        jax.ShapeDtypeStruct((2, WR, QC), BF),
        jax.ShapeDtypeStruct((40, 8192), BF),
    )
    results = pl.pallas_call(
        kernel,
        out_shape=shapes,
        in_specs=[anywhere] * 6,
        out_specs=(vm, vm, vm, vm),
        scratch_shapes=[
            pltpu.VMEM((L, QC), BF),
            pltpu.VMEM((L, HD), F32),
            pltpu.VMEM((L, HD), F32),
            pltpu.VMEM((L, 8192), BF),
            pltpu.VMEM((NZ, 4, WR, C1), BF),
            pltpu.VMEM((NZ, 4, WR, WC - C1), BF),
            pltpu.VMEM((L, WC), F32),
            pltpu.VMEM((L, HD), F32),
            pltpu.VMEM((L, HD), F32),
            pltpu.VMEM((L, C1), BF),
            pltpu.VMEM((L, WC - C1), BF),
            pltpu.VMEM((L, HD), BF),
            pltpu.VMEM((L, HD), BF),
            pltpu.VMEM((WC + HD, L), BF),
            pltpu.VMEM((HEADS, L, HD), BF),
            pltpu.VMEM((HEADS, L, 2 * HD), BF),
            pltpu.VMEM((L, 2 * HD), BF),
            pltpu.VMEM((L, HD), BF),
            pltpu.VMEM((2, L, L), BF),
            pltpu.VMEM((L, HD), F32),
            pltpu.VMEM((L, HD), F32),
            pltpu.VMEM((NZ, 2, 2, WC, WR), BF),
            pltpu.VMEM((NZ, 2, WC, WR), BF),
            pltpu.VMEM((4, 2, 2, WC, WR), BF),
            pltpu.VMEM((NZ, HD, WR), BF),
            pltpu.VMEM((4 * HD, WR), BF),
            pltpu.VMEM((4 * HD, WR), BF),
            pltpu.VMEM((DIRECT, 4, 2, 80, 512), BF),
            pltpu.VMEM((DIRECT, 2, 80, 512), BF),
            pltpu.VMEM((DIRECT, 2, 2, 80, 512), BF),
            pltpu.VMEM((DIRECT, 80, 512), F32),
            pltpu.VMEM((DIRECT, 80, 512), BF),
            pltpu.VMEM((DIRECT, 80, 512), BF),
            pltpu.VMEM((max(8 - DIRECT, 1), 2, 4, 80, 512), BF),
            pltpu.VMEM((max(8 - DIRECT, 1), 4, 80, 512), BF),
            pltpu.VMEM((max(8 - DIRECT, 1), 2, 80, 256), BF),
            pltpu.VMEM((max(8 - DIRECT, 1), 2, 80, 512), BF),
            pltpu.VMEM((8, WR, HD), BF),
            dma((7,)),
            dma((2, 3, 2, 5)), dma((2, 3, 2, 5)),
            dma((2, 2, 2, 5)), dma((2, 2, 2, 5)),
            dma((2, 4, 2, 5)), dma((2, 4, 2, 5)),
            dma((2,)), dma((2,)),
            dma((2, 8)), dma((2, 8)),
            dma((8,)), dma((8,)),
            dma((4, 5, 2)), dma((4, 5, 2)),
            dma((2,)), dma((2,)),
            dma((8, 2)), dma((8, 2)),
            dma((8, 2)), dma((8, 2)),
            dma((8,)), dma((8,)),
            dma((7,)), dma((8,)),
        ],
        compiler_params=pltpu.CompilerParams(
            collective_id=0, has_side_effects=True, vmem_limit_bytes=60 * 2**20
        ),
        cost_estimate=pl.CostEstimate(
            flops=14_000_000_000, bytes_accessed=8_000_000, transcendentals=410_000
        ),
        name="attention_step",
    )(inputs, query_weight, kv_weight, out_grad, cos, sin)
    return pl.pallas_call(
        place,
        out_shape=shapes,
        in_specs=[anywhere] * 4,
        out_specs=(anywhere,) * 4,
        scratch_shapes=[pltpu.VMEM(s.shape, s.dtype) for s in shapes] + [dma((2, 4))],
        name="place",
    )(*results)


def solution(mesh):
    return jax.shard_map(
        per_device,
        mesh=mesh,
        in_specs=(P("blk", None), P("blk", "tensor"), P(None, "blk", None), P("blk", "tensor")),
        out_specs=(
            P("blk", "tensor"),
            P("blk", "tensor"),
            P(None, "blk", None),
            P(("blk", "tensor"), None),
        ),
        check_vma=False,
    )
```

```python
import functools
import math

import jax
import jax.numpy as jnp
import numpy as np
from jax import lax
from jax.experimental import pallas as pl
from jax.experimental.pallas import tpu as pltpu
from jax.sharding import PartitionSpec as P

HD = 128
HEADS = 4
L = 320
NZ = 8
WR = 256
WC = 640
QC = 512
AF = 128
C1 = 384
DIRECT = 6
MESH = pl.DeviceIdType.MESH
BF = jnp.bfloat16
F32 = jnp.float32
NT = (((1,), (1,)), ((), ()))
NN = (((1,), (0,)), ((), ()))
SCALE = 1.0 / math.sqrt(HD)
SGN = (1, -1)


PLAN = (
    ("P", 1, 4), ("PR", 2), ("T4",), ("PR", 3), ("S", 1, 4), ("Z", 0, "O", 1), ("Z", 0, "N", 1),
    ("P", 1, -2), ("Z", 0, "O", 0), ("Z", 0, "N", 0), ("PR", 4), ("H", 2), ("H", 3), ("HS",),
    ("P", 1, 3), ("QG", 3), ("P", 1, -3), ("P", 1, 2), ("S", 1, 3), ("P", 1, 1), ("QG", 2),
    ("Z", 1, "N", 0), ("S", 1, -3), ("Z", 1, "O", 0), ("Z", 1, "O", 1), ("S", 1, -2),
    ("Z", 1, "N", 1), ("S", 1, 2), ("KV",), ("D", 6), ("D", 3), ("P", 2, 4), ("D", 4), ("D", 5),
    ("P", 2, -2), ("S", 2, 4), ("Z", 0, "Q", 1), ("P", 2, -3), ("D", 1), ("Z", 0, "Q", 0),
    ("Z", 0, "M", 0), ("P", 2, 3), ("Z", 2, "O", 1), ("Z", 0, "M", 1), ("S", 2, -2), ("Y", 3, 1),
    ("Y", 3, 0), ("S", 2, -3), ("P", 2, -1), ("Y", 4, 1), ("Z", 2, "O", 0), ("P", 1, -1),
    ("S", 2, 3), ("Z", 1, "Q", 1), ("S", 1, 1), ("Y", 5, 0), ("D", 7), ("Y", 5, 1),
    ("Z", 1, "Q", 0), ("D", 2), ("P", 2, 2), ("A", 2, 4), ("Z", 0, "K", 0), ("S", 1, -1),
    ("Z", 1, "M", 0), ("Z", 0, "K", 1), ("P", 2, 0), ("P", 2, 1), ("Z", 1, "M", 1), ("A", 2, -2),
    ("Y", 1, 1), ("Y", 4, 0), ("A", 2, -3), ("D", 0), ("Z", 3, "O", 0), ("Z", 1, "K", 1),
    ("A", 2, 3), ("S", 2, 1), ("Y", 1, 0), ("Z", 1, "K", 0), ("Z", 3, "O", 1), ("S", 2, 2),
    ("S", 2, -1), ("Z", 2, "Q", 0), ("YL", 3), ("P", 1, 0), ("Z", 2, "Q", 1), ("LQ", 7),
    ("Z", 2, "M", 0), ("LQ", 6), ("S", 1, 0), ("Y", 2, 1), ("Z", 2, "K", 1), ("Y", 2, 0),
    ("YL", 5), ("S", 2, 0), ("ZL", "O"), ("Z", 2, "M", 1), ("A", 2, 1), ("YL", 4), ("A", 2, 2),
    ("Z", 2, "K", 0), ("Z", 3, "Q", 1), ("YQ", 7, 0), ("A", 2, -1), ("LL", 3), ("Z", 3, "Q", 0),
    ("Z", 3, "K", 1), ("YQ", 6, 0), ("YQ", 7, 1), ("Y", 0, 0), ("YL", 1), ("Y", 0, 1),
    ("Z", 2, "N", 1), ("YQ", 6, 1), ("Z", 3, "K", 0), ("Z", 2, "N", 0), ("Z", 3, "M", 0),
    ("Z", 3, "M", 1), ("YL", 2), ("ZL", "Q"), ("A", 2, 0), ("ZL", "K"), ("LL", 4), ("FQ", 7),
    ("Z", 3, "N", 0), ("Z", 3, "N", 1), ("YL", 0), ("FQ", 6), ("LL", 5), ("LL", 2), ("LL", 1),
    ("ZL", "M"), ("ZL", "N"), ("FIN",), ("LL", 0),
)


def dot(a, b, dims=NN):
    return lax.dot_general(a, b, dims, preferred_element_type=F32)


def kernel(
    x_hbm, wq_hbm, kv_hbm, do_hbm, cos_hbm, sin_hbm,
    att_ref, dwq_ref, dkv_ref, dx_ref,
    do_ref, cos_ref, sin_ref, xv, wg1, wg2, acc, kvs, kvr, g1, g2, gother, gsend, gt,
    qh_s, qcat, kcat, vb_s, ds_s, dk_s, dv_s, pw, rc, rz, rxf, xfs, xfr,
    dxp, ry0, ry1, keep, ls, rl, dxq, rlq, ry0q, ry1q, kvb,
    lsem, zs, zr, xs, xr, cs, cr, es, er,
    pcs, pcr, pxs, pxr, pzs, pzr, pfs, pfr, y0s, y0r, y1s, y1r, lls, llr, ks, kr,
):
    blk = lax.axis_index("blk")
    t = lax.axis_index("tensor")
    z, h, c = blk // 4, (blk // 2) % 2, blk % 2
    y, l = t // 2, t % 2

    def dev(zz, hh, cc, yy, ll):
        return (zz * 4 + hh * 2 + cc, yy * 2 + ll)

    znb = (dev((z + 1) % NZ, h, c, y, l), dev((z + NZ - 1) % NZ, h, c, y, l))
    ynb = (dev(z, h, c, (y + 1) % 4, l), dev(z, h, c, (y + 3) % 4, l))
    xpeer = dev(z, 1 - h, c, y, l)
    cpeer = dev(z, h, 1 - c, y, l)
    lpeer = dev(z, h, c, y, 1 - l)
    tpeers = [(blk, (t + k) % 8) for k in range(1, 8)]

    sends = []

    def send(src, dst, ssem, rsem, peer):
        copy = pltpu.make_async_remote_copy(
            src_ref=src, dst_ref=dst, send_sem=ssem, recv_sem=rsem,
            device_id=peer, device_id_type=MESH,
        )
        copy.start()
        sends.append(copy)

    def arrived(ref, ssem, rsem, peer):
        pltpu.make_async_remote_copy(
            src_ref=ref, dst_ref=ref, send_sem=ssem, recv_sem=rsem,
            device_id=peer, device_id_type=MESH,
        ).wait_recv()

    own = h * 2 + c
    oth = (1 - h) * 2 + c
    loads = [
        pltpu.make_async_copy(src, dst, lsem.at[i])
        for i, (src, dst) in enumerate((
            (wq_hbm.at[:, pl.ds(0, C1 - HD)], wg1.at[z, own, :, pl.ds(HD, C1 - HD)]),
            (wq_hbm.at[:, pl.ds(C1 - HD, WC - C1)], wg2.at[z, own]),
            (
                kv_hbm.at[l, :, pl.ds(pl.multiple_of(y * HD, HD), HD)],
                wg1.at[z, own, :, pl.ds(0, HD)],
            ),
            (x_hbm, xv),
            (do_hbm, do_ref),
            (cos_hbm, cos_ref),
            (sin_hbm, sin_ref),
        ))
    ]
    for copy in loads:
        copy.start()

    barrier = pltpu.get_barrier_semaphore()
    greet = [znb[0], znb[1], xpeer, cpeer] + tpeers
    for peer in greet:
        pl.semaphore_signal(barrier, inc=1, device_id=peer, device_id_type=MESH)
    acc[...] = jnp.zeros_like(acc)
    for copy in loads[:3]:
        copy.wait()
    pl.semaphore_wait(barrier, len(greet))

    def slot(d, k):
        return (z + 2 * NZ - SGN[k] * d) % NZ

    piece = {"A": 0, "B": 1, "O": 2, "X": 3}
    column = {"A": own, "B": own, "O": oth, "X": oth}

    class Gather:
        def __init__(self, g, buf, split, low, width):
            self.g, self.buf, self.split = g, buf, split
            self.cols = pl.ds(low, width)

        def rows(self, p, d, k):
            f = self.split
            if p in "AX":
                return pl.ds(0, f) if f > 0 and (d < 4 or k == 0) else None
            n = WR - f
            if d < 4:
                return pl.ds(f, n)
            if p == "B" and f > 0:
                return pl.ds(f, n) if k == 1 else None
            return pl.ds(f + k * (n // 2), n // 2)

        def part(self, p, d, k):
            r = self.rows(p, d, k)
            return None if r is None else self.buf.at[slot(d, k), column[p], r]

        def z_send(self, p, d, k):
            r = self.rows(p, d, k)
            if r is not None:
                ref = self.buf.at[slot(d - 1, k), column[p], r]
                at = (self.g, piece[p], k, d)
                send(ref, ref, zs.at[at], zr.at[at], znb[k])

        def x_send(self, p, d, k, ref):
            at = (self.g, piece[p], k, d)
            send(ref, ref, xs.at[at], xr.at[at], xpeer)

        def to_core(self, p, d, k, ref):
            at = (self.g, piece[p], k, d)
            send(ref, ref, cs.at[at], cr.at[at], cpeer)

        def start(self):
            for p in "AB":
                ref = self.part(p, 0, 0)
                if ref is not None:
                    for k in (0, 1):
                        self.z_send(p, 1, k)

        def start_x(self):
            for p in "BA":
                ref = self.part(p, 0, 0)
                if ref is not None:
                    self.x_send(p, 0, 0, ref)
                    self.to_core(p, 0, 0, ref)

        def start_other(self):
            ref = self.part("O", 0, 0)
            at = (self.g, 1, 0, 0)
            arrived(ref, xs.at[at], xr.at[at], xpeer)
            for k in (0, 1):
                self.z_send("O", 1, k)
            self.to_core("O", 0, 0, ref)

        def tick(self, p, d):
            for k in (0, 1):
                ref = self.part(p, d, k)
                if ref is None:
                    continue
                at = (self.g, piece[p], k, d)
                arrived(ref, zs.at[at], zr.at[at], znb[1 - k])
                if d < 4:
                    self.z_send(p, d + 1, k)
                if p == "A":
                    self.x_send("A", d, k, ref)
                self.to_core(p, d, k, ref)

        def from_x(self, d):
            for k in (0, 1):
                ref = self.part("X", d, k)
                if ref is not None and (d > 0 or k == 0):
                    at = (self.g, 0, k, d)
                    arrived(ref, xs.at[at], xr.at[at], xpeer)
                    self.to_core("X", d, k, ref)

        def from_core(self, d, k):
            zp = slot(d, k)
            for p, hc in (("A", h * 2), ("B", h * 2), ("O", 2 - h * 2), ("X", 2 - h * 2)):
                r = self.rows(p, d, k)
                if r is not None:
                    at = (self.g, piece[p], k, d)
                    arrived(self.buf.at[zp, hc + 1 - c, r], cs.at[at], cr.at[at], cpeer)

        def proj(self, d, k):
            self.from_core(d, k)
            if d == 4:
                self.from_core(d, 1 - k)
            zp = slot(d, k)
            xcols = xv[:, pl.ds(pl.multiple_of(zp * 1024, 1024), 1024)]
            w = self.buf[zp]
            acc[:, self.cols] += dot(xcols, w.reshape(4 * WR, w.shape[-1]))

    one = Gather(0, wg1, AF, 0, C1)
    two = Gather(1, wg2, 0, C1, WC - C1)

    one.start()
    one.start_x()
    one.start_other()
    one.tick("A", 1)
    one.from_x(0)
    one.tick("B", 1)
    two.start_x()
    loads[3].wait()
    one.proj(0, 0)
    one.tick("O", 1)
    for d in (2, 3):
        one.tick("A", d)
        one.from_x(d - 1)
        one.tick("B", d)
        one.proj(d - 1, 0)
        one.tick("O", d)
        one.proj(d - 1, 1)
    two.start()
    two.start_other()
    one.tick("A", 4)
    one.from_x(3)
    one.tick("B", 4)
    one.proj(3, 0)
    one.tick("O", 4)
    one.proj(3, 1)
    two.tick("B", 1)
    two.tick("O", 1)
    one.from_x(4)
    one.proj(4, 0)

    kvs[...] = acc[:, :HD]
    send(kvs, kvr, es.at[0], er.at[0], lpeer)
    for copy in loads[4:]:
        copy.wait()
    cosv = cos_ref[...]
    sinv = sin_ref[...]

    def rot(v):
        return v * cosv + pltpu.roll(v, HD // 2, 1) * sinv

    def unrot(v):
        return v * cosv - pltpu.roll(v, HD // 2, 1) * sinv

    def queries(g):
        qr = rot(acc[:, pl.ds(HD + g * HD, HD)])
        qs = qr * SCALE
        qsh = qs.astype(BF)
        qcat[g, :, pl.ds(0, HD)] = qsh
        qcat[g, :, pl.ds(HD, HD)] = (qs - qsh.astype(F32)).astype(BF)
        qh_s[g] = qr.astype(BF)

    two.proj(0, 0)
    two.tick("B", 2)
    two.tick("O", 2)
    queries(0)
    queries(1)
    two.proj(1, 0)
    two.proj(1, 1)
    two.tick("B", 3)
    two.tick("O", 3)
    arrived(kvr, es.at[0], er.at[0], lpeer)
    first = l == 0
    kr_f = rot(jnp.where(first, kvs[...], kvr[...]))
    kh = kr_f.astype(BF)
    kcat[:, pl.ds(0, HD)] = kh
    kcat[:, pl.ds(HD, HD)] = (kr_f - kh.astype(F32)).astype(BF)
    vb_s[...] = jnp.where(first, kvr[...], kvs[...]).astype(BF)

    def head(g):
        cols = pl.ds(g * HD, HD)
        vb = vb_s[...]
        qsh, qsl = qcat[g, :, :HD], qcat[g, :, HD:]
        khv, klv = kcat[:, :HD], kcat[:, HD:]
        s = dot(
            jnp.concatenate([qsh, qsh, qsl], axis=1),
            jnp.concatenate([khv, klv, khv], axis=1), NT,
        )
        allowed = lax.broadcasted_iota(jnp.int32, (L, L), 1) <= lax.broadcasted_iota(
            jnp.int32, (L, L), 0
        )
        s = jnp.where(allowed, s, -1e30)
        e = jnp.exp(s - jnp.max(s, axis=1, keepdims=True))
        p = e / jnp.sum(e, axis=1, keepdims=True)
        pb = p.astype(BF)
        dob = do_ref[:, cols]
        att_ref[:, cols] = dot(pb, vb).astype(BF)
        dp = dot(dob, vb, NT)
        dsb = (p * (dp - jnp.sum(p * dp, axis=1, keepdims=True))).astype(BF)
        ds_s[g % 2] = dsb
        dk, dv = dot(dsb.T, qh_s[g]), dot(pb.T, dob)
        if g == 0:
            dk_s[...] = dk
            dv_s[...] = dv
        else:
            dk_s[...] += dk
            dv_s[...] += dv

    def query_grad(g):
        dq = unrot(dot(ds_s[g % 2], kcat[:, :HD]) * SCALE)
        if g < 2:
            g1[:, pl.ds(HD + g * HD, HD)] = dq.astype(BF)
        else:
            g2[:, pl.ds((g - 2) * HD, HD)] = dq.astype(BF)
        gt[pl.ds((g if g < 2 else g + 1) * HD, HD), :] = dq.T.astype(BF)

    head(0)
    head(1)
    query_grad(0)
    query_grad(1)

    def last_tick():
        two.tick("B", 4)
        two.tick("O", 4)

    def projections(d):
        two.proj(d, 0)
        if d < 4:
            two.proj(d, 1)
        else:
            queries(2)
            queries(3)

    def send_kv_grad():
        dk, dv = unrot(dk_s[...] * SCALE), dv_s[...]
        gsend[...] = jnp.where(first, dv, dk).astype(BF)
        send(gsend, gother, es.at[1], er.at[1], lpeer)
        mine = jnp.where(first, dk, dv)
        g1[:, pl.ds(0, HD)] = mine.astype(BF)
        gt[pl.ds(2 * HD, HD), :] = mine.T.astype(BF)

    def kv_grad():
        arrived(gother, es.at[1], er.at[1], lpeer)
        gt[pl.ds(WC, HD), :] = gother[...].astype(F32).T.astype(BF)

    pieces = {
        "N": (0, 0, 2 * HD), "O": (1, 0, 2 * HD),
        "K": (0, 2 * HD, HD), "M": (0, 3 * HD, 2 * HD), "Q": (1, 3 * HD, 2 * HD),
    }
    order = {p: i for i, p in enumerate(pieces)}
    group_rows = {1: (0, 2 * HD), 2: (2 * HD, 3 * HD)}

    def add(dst, src, base, n, step, shift=0):
        def body(i, carry):
            at = pl.multiple_of(base + i * step, 16)
            r = pl.ds(at, step)
            dst[r, :] = dst[r, :] + src[pl.ds(pl.multiple_of(at - shift, 16), step), :]
            return carry

        lax.fori_loop(0, n // step, body, 0)

    def zat(o):
        return (z + NZ + o) % NZ

    def products(g, o):
        zp = zat(o)

        def body(j, carry):
            xcols = xv[:, pl.ds(pl.multiple_of(zp * 1024 + j * WR, WR), WR)]
            cc, hh = j % 2, j // 2
            if g == 1:
                pw[zp, cc, hh, pl.ds(0, 256), :] = dot(gt[pl.ds(0, 256), :], xcols).astype(BF)
            else:
                both = dot(gt[pl.ds(256, HD), :], xcols) + dot(gt[pl.ds(WC, HD), :], xcols)
                pw[zp, cc, hh, pl.ds(256, HD), :] = both.astype(BF)
                pw[zp, cc, hh, pl.ds(384, 256), :] = dot(
                    gt[pl.ds(384, 256), :], xcols
                ).astype(BF)
            return carry

        lax.fori_loop(0, 4, body, 0)
        i = o % NZ
        r = pl.ds(*group_rows[g])
        at = (g - 1, i)
        send(pw.at[zp, 1 - c, :, r], rc.at[i, :, r], pcs.at[at], pcr.at[at], cpeer)

    def core_sum(g, o):
        zp, i = zat(o), o % NZ
        low, n = group_rows[g]
        r = pl.ds(low, n)
        at = (g - 1, i)
        arrived(rc.at[i, :, r], pcs.at[at], pcr.at[at], cpeer)
        add(pw.at[zp, c, 1 - h], rc.at[i, 1 - h], low, n, 128)
        if g == 2:
            part = pw.at[zp, c, 1 - h, pl.ds(low, HD)]
            send(part, rxf.at[i], pxs.at[i], pxr.at[i], xpeer)
        add(pw.at[zp, c, h], rc.at[i, h], low, n, 128)

    def x_sum(g, o):
        zp, i = zat(o), o % NZ
        arrived(rxf.at[i], pxs.at[i], pxr.at[i], xpeer)
        low = group_rows[g][0]
        add(pw.at[zp, c, h], rxf.at[i], low, HD, 128, low)

    def z_rows(s, p, k):
        base, n = pieces[p][1:]
        return (base, n) if s > 0 else (base + k * (n // 2), n // 2)

    def z_arrived(s, p, k):
        base, n = z_rows(s, p, k)
        ring, i = pieces[p][0], order[p]
        arrived(
            rz.at[s, ring, k, pl.ds(base, n)], pzs.at[s, i, k], pzr.at[s, i, k], znb[1 - k]
        )

    def z_step(s, p, k):
        ring, i = pieces[p][0], order[p]
        hh = 1 - h if ring else h
        zp = zat(SGN[k] * (4 - s))
        if s > 0:
            z_arrived(s - 1, p, k)
            base, n = z_rows(s - 1, p, k)
            add(pw.at[zp, c, hh], rz.at[s - 1, ring, k], base, n, 64)
        base, n = z_rows(s, p, k)
        send(
            pw.at[zp, c, hh, pl.ds(base, n)], rz.at[s, ring, k, pl.ds(base, n)],
            pzs.at[s, i, k], pzr.at[s, i, k], znb[k],
        )

    def total(r, ring):
        rows = pl.ds(r, 128)
        return (
            pw[z, c, 1 - h if ring else h, rows, :].astype(F32)
            + rz[3, ring, 0, rows, :].astype(F32)
            + rz[3, ring, 1, rows, :].astype(F32)
        )

    last = {"O": (0, 0), "N": (0, 0), "Q": (1, 2 * HD), "M": (1, 2 * HD)}

    def z_last(p):
        z_arrived(3, p, 0)
        z_arrived(3, p, 1)
        ring, base, n = pieces[p]
        if p == "K":
            kvb[t] = total(base, 0).T.astype(BF)
            for k, peer in enumerate(tpeers):
                send(kvb.at[t], kvb.at[t], ks.at[k], kr.at[t], peer)
            return
        if p in last:
            i, at = last[p]
        if p in "OQ":
            for r in range(0, n, 128):
                xfs[pl.ds(at + r, 128), :] = total(base + r, 1).astype(BF)
            rows = pl.ds(at, n)
            send(xfs.at[rows], xfr.at[rows], pfs.at[i], pfr.at[i], xpeer)
            return
        if p in "NM":
            arrived(xfr.at[pl.ds(at, n)], pfs.at[i], pfr.at[i], xpeer)
        for r in range(0, n, 128):
            s = total(base + r, 0)
            if p in "NM":
                s = s + xfr[pl.ds(at + r, 128), :].astype(F32)
            low = base + r if base < 256 else base + r - HD
            dwq_ref[:, pl.ds(low, 128)] = s.T.astype(BF)

    def dx_products(i):
        halves = []
        for hf in (0, 1):
            wa = wg1[i, 2 * hf:2 * hf + 2].reshape(2 * WR, C1)
            wb = wg2[i, 2 * hf:2 * hf + 2].reshape(2 * WR, WC - C1)
            r = dot(g1[...], wa, NT) + dot(gother[...], wa[:, :HD], NT) + dot(g2[...], wb, NT)
            if i < DIRECT:
                dxp[i, :, hf] = r.reshape(4, 80, 512).astype(BF)
            else:
                halves.append(r.reshape(4, 2, 40, 512))
        if i < DIRECT:
            for k in (0, 1):
                send(
                    dxp.at[i, (y + 2) % 4, k], ry0.at[i, k], y0s.at[i, k], y0r.at[i, k],
                    ynb[k],
                )
            return
        j = i - DIRECT
        for ll in (0, 1):
            both = jnp.concatenate([halves[0][:, ll], halves[1][:, ll]], axis=1)
            dxq[j, ll] = both.astype(BF)
        send(dxq.at[j, 1 - l], rlq.at[j], lls.at[i], llr.at[i], lpeer)

    def lq_step(i):
        j = i - DIRECT
        arrived(rlq.at[j], lls.at[i], llr.at[i], lpeer)
        dxq[j, l] = dxq[j, l] + rlq[j]
        for k in (0, 1):
            send(
                dxq.at[j, l, (y + 2) % 4, :, pl.ds(k * 256, 256)], ry0q.at[j, k],
                y0s.at[i, k], y0r.at[i, k], ynb[k],
            )

    def yq_step(i, k):
        j = i - DIRECT
        arrived(ry0q.at[j, k], y0s.at[i, k], y0r.at[i, k], ynb[1 - k])
        yy = (y + 4 + SGN[k]) % 4
        lanes = pl.ds(k * 256, 256)
        dxq[j, l, yy, :, lanes] = dxq[j, l, yy, :, lanes] + ry0q[j, k]
        send(dxq.at[j, l, yy], ry1q.at[j, k], y1s.at[i, k], y1r.at[i, k], ynb[k])

    def yq_last(i):
        j = i - DIRECT
        for k in (0, 1):
            arrived(ry1q.at[j, k], y1s.at[i, k], y1r.at[i, k], ynb[1 - k])
        s = dxq[j, l, y].astype(F32) + ry1q[j, 0].astype(F32) + ry1q[j, 1].astype(F32)
        dx_ref[:, pl.ds(i * 1024, 512)] = s[:40].astype(BF)
        dx_ref[:, pl.ds(i * 1024 + 512, 512)] = s[40:].astype(BF)

    def y_step(i, k):
        arrived(ry0.at[i, k], y0s.at[i, k], y0r.at[i, k], ynb[1 - k])
        yy = (y + 4 + SGN[k]) % 4
        dxp[i, yy, k] = dxp[i, yy, k] + ry0[i, k]
        send(dxp.at[i, yy], ry1.at[i, k], y1s.at[i, k], y1r.at[i, k], ynb[k])

    def y_last(i):
        for k in (0, 1):
            arrived(ry1.at[i, k], y1s.at[i, k], y1r.at[i, k], ynb[1 - k])
        s = dxp[i, y].astype(F32) + ry1[i, 0].astype(F32) + ry1[i, 1].astype(F32)
        a = jnp.concatenate([s[0, :40], s[1, :40]], axis=0)
        b = jnp.concatenate([s[0, 40:], s[1, 40:]], axis=0)
        keep[i] = jnp.where(first, a, b)
        ls[i] = jnp.where(first, b, a).astype(BF)
        send(ls.at[i], rl.at[i], lls.at[i], llr.at[i], lpeer)

    def l_last(i):
        arrived(rl.at[i], lls.at[i], llr.at[i], lpeer)
        s = (keep[i] + rl[i].astype(F32)).astype(BF)
        dx_ref[:, pl.ds(i * 1024, 512)] = s[:40]
        dx_ref[:, pl.ds(i * 1024 + 512, 512)] = s[40:]

    def kv_last():
        for k, peer in enumerate(tpeers):
            tt = (t + 1 + k) % 8
            arrived(kvb.at[tt], ks.at[k], kr.at[tt], peer)
        for yy in range(4):
            for ll in range(2):
                dkv_ref[ll, :, pl.ds(yy * HD, HD)] = kvb[yy * 2 + ll]

    steps = {
        "P": products, "S": core_sum, "A": x_sum, "Z": z_step, "ZL": z_last,
        "D": dx_products, "Y": y_step, "YL": y_last, "LL": l_last, "FIN": kv_last,
        "LQ": lq_step, "YQ": yq_step, "FQ": yq_last, "T4": last_tick, "PR": projections,
        "H": head, "HS": send_kv_grad, "QG": query_grad, "KV": kv_grad,
    }
    for name, *which in PLAN:
        steps[name](*which)
    for copy in sends:
        copy.wait_send()


def tables():
    i = np.arange(HD // 2, dtype=np.float64)
    ang = np.arange(L, dtype=np.float64)[:, None] * np.exp(i * (-2.0 * math.log(10000.0) / HD))
    cos, sin = np.cos(ang), np.sin(ang)
    return (
        np.concatenate([cos, cos], axis=1).astype(np.float32),
        np.concatenate([-sin, sin], axis=1).astype(np.float32),
    )


def place(a, b, c, d, oa, ob, oc, od, va, vb, vc, vd, sem):
    ways = ((a, va, oa), (b, vb, ob), (c, vc, oc), (d, vd, od))
    into = [pltpu.make_async_copy(src, mid, sem.at[0, i]) for i, (src, mid, _) in enumerate(ways)]
    out = [pltpu.make_async_copy(mid, dst, sem.at[1, i]) for i, (_, mid, dst) in enumerate(ways)]
    for copy in into:
        copy.start()
    for first, second in zip(into, out):
        first.wait()
        second.start()
    for copy in out:
        copy.wait()


def per_device(inputs, query_weight, kv_weight, out_grad):
    cos, sin = tables()
    vm = pl.BlockSpec(memory_space=pltpu.VMEM)
    anywhere = pl.BlockSpec(memory_space=pl.ANY)
    dma = pltpu.SemaphoreType.DMA
    shapes = (
        jax.ShapeDtypeStruct((L, QC), BF),
        jax.ShapeDtypeStruct((WR, QC), BF),
        jax.ShapeDtypeStruct((2, WR, QC), BF),
        jax.ShapeDtypeStruct((40, 8192), BF),
    )
    results = pl.pallas_call(
        kernel,
        out_shape=shapes,
        in_specs=[anywhere] * 6,
        out_specs=(vm, vm, vm, vm),
        scratch_shapes=[
            pltpu.VMEM((L, QC), BF),
            pltpu.VMEM((L, HD), F32),
            pltpu.VMEM((L, HD), F32),
            pltpu.VMEM((L, 8192), BF),
            pltpu.VMEM((NZ, 4, WR, C1), BF),
            pltpu.VMEM((NZ, 4, WR, WC - C1), BF),
            pltpu.VMEM((L, WC), F32),
            pltpu.VMEM((L, HD), F32),
            pltpu.VMEM((L, HD), F32),
            pltpu.VMEM((L, C1), BF),
            pltpu.VMEM((L, WC - C1), BF),
            pltpu.VMEM((L, HD), BF),
            pltpu.VMEM((L, HD), BF),
            pltpu.VMEM((WC + HD, L), BF),
            pltpu.VMEM((HEADS, L, HD), BF),
            pltpu.VMEM((HEADS, L, 2 * HD), BF),
            pltpu.VMEM((L, 2 * HD), BF),
            pltpu.VMEM((L, HD), BF),
            pltpu.VMEM((2, L, L), BF),
            pltpu.VMEM((L, HD), F32),
            pltpu.VMEM((L, HD), F32),
            pltpu.VMEM((NZ, 2, 2, WC, WR), BF),
            pltpu.VMEM((NZ, 2, WC, WR), BF),
            pltpu.VMEM((4, 2, 2, WC, WR), BF),
            pltpu.VMEM((NZ, HD, WR), BF),
            pltpu.VMEM((4 * HD, WR), BF),
            pltpu.VMEM((4 * HD, WR), BF),
            pltpu.VMEM((DIRECT, 4, 2, 80, 512), BF),
            pltpu.VMEM((DIRECT, 2, 80, 512), BF),
            pltpu.VMEM((DIRECT, 2, 2, 80, 512), BF),
            pltpu.VMEM((DIRECT, 80, 512), F32),
            pltpu.VMEM((DIRECT, 80, 512), BF),
            pltpu.VMEM((DIRECT, 80, 512), BF),
            pltpu.VMEM((max(8 - DIRECT, 1), 2, 4, 80, 512), BF),
            pltpu.VMEM((max(8 - DIRECT, 1), 4, 80, 512), BF),
            pltpu.VMEM((max(8 - DIRECT, 1), 2, 80, 256), BF),
            pltpu.VMEM((max(8 - DIRECT, 1), 2, 80, 512), BF),
            pltpu.VMEM((8, WR, HD), BF),
            dma((7,)),
            dma((2, 3, 2, 5)), dma((2, 3, 2, 5)),
            dma((2, 2, 2, 5)), dma((2, 2, 2, 5)),
            dma((2, 4, 2, 5)), dma((2, 4, 2, 5)),
            dma((2,)), dma((2,)),
            dma((2, 8)), dma((2, 8)),
            dma((8,)), dma((8,)),
            dma((4, 5, 2)), dma((4, 5, 2)),
            dma((2,)), dma((2,)),
            dma((8, 2)), dma((8, 2)),
            dma((8, 2)), dma((8, 2)),
            dma((8,)), dma((8,)),
            dma((7,)), dma((8,)),
        ],
        compiler_params=pltpu.CompilerParams(
            collective_id=0, has_side_effects=True, vmem_limit_bytes=60 * 2**20
        ),
        cost_estimate=pl.CostEstimate(
            flops=14_000_000_000, bytes_accessed=8_000_000, transcendentals=410_000
        ),
        name="attention_step",
    )(inputs, query_weight, kv_weight, out_grad, cos, sin)
    return pl.pallas_call(
        place,
        out_shape=shapes,
        in_specs=[anywhere] * 4,
        out_specs=(anywhere,) * 4,
        scratch_shapes=[pltpu.VMEM(s.shape, s.dtype) for s in shapes] + [dma((2, 4))],
        name="place",
    )(*results)


def solution(mesh):
    return jax.shard_map(
        per_device,
        mesh=mesh,
        in_specs=(P("blk", None), P("blk", "tensor"), P(None, "blk", None), P("blk", "tensor")),
        out_specs=(
            P("blk", "tensor"),
            P("blk", "tensor"),
            P(None, "blk", None),
            P(("blk", "tensor"), None),
        ),
        check_vma=False,
    )
```
